32 devices in a mesh: dp: 8 (over z, y), ctx: 4 (over x, core).
Axes of the slice: x: 2, y: 2, z: 4, core: 2. Of those that a mesh axis runs over, the one named last changes fastest.
Arguments:
- layer_input: float32 [8, 512, 1024], P('dp', 'ctx'), may hold values from -6 to 6
- segment_ids: int32 [8, 512], P('dp'), may hold values from 0 to 2, never falling along the last dimension, each value on 1 to 384 neighbouring positions
- ln1_gain: float32 [1024], replicated, may hold values from 0.1 to 1.9
- ln1_bias: float32 [1024], replicated, may hold values from -3 to 3
- w_qkv: bfloat16 [1024, 3072], P('dp', 'ctx')
- qv_bias: float32 [2048], replicated, may hold values from -3 to 3
- w_out: bfloat16 [1024, 1024], P('dp', 'ctx'), may hold values from -0.75 to 0.75
- out_bias: float32 [1024], replicated, may hold values from -3 to 3
- ln2_gain: float32 [1024], replicated, may hold values from 0.1 to 1.9
- ln2_bias: float32 [1024], replicated, may hold values from -3 to 3
- w_up: bfloat16 [1024, 4096], P('dp', 'ctx'), may hold values from -0.1875 to 0.1875
- up_bias: float32 [4096], replicated, may hold values from -3 to 3
- w_down: bfloat16 [4096, 1024], P('dp', 'ctx'), may hold values from -0.09375 to 0.09375
- down_bias: float32 [1024], replicated, may hold values from -3 to 3
- cotangent: float32 [8, 512, 1024], P('dp', 'ctx'), may hold values from -6 to 6
Outputs:
- result: float32 [8, 512, 1024], P('dp', 'ctx')
- input_grad: float32 [8, 512, 1024], P('dp', 'ctx')
- ln1_gain_grad: float32 [1024], replicated
- ln1_bias_grad: float32 [1024], replicated
- w_qkv_grad: float32 [1024, 3072], P('dp', 'ctx')
- qv_bias_grad: float32 [2048], replicated
- w_out_grad: float32 [1024, 1024], P('dp', 'ctx')
- out_bias_grad: float32 [1024], replicated
- ln2_gain_grad: float32 [1024], replicated
- ln2_bias_grad: float32 [1024], replicated
- w_up_grad: float32 [1024, 4096], P('dp', 'ctx')
- up_bias_grad: float32 [4096], replicated
- w_down_grad: float32 [4096, 1024], P('dp', 'ctx')
- down_bias_grad: float32 [1024], replicated
The draws below stay inside these ranges and needn't reach their ends.
Inputs may be any that keep to these rules, and one draw needn't show every extreme that they name: `segment_ids`: segment ids never fall along a sequence; every document holds 1 to 384 tokens and one of each sequence holds exactly that many.
All inputs are finite; a program needn't handle non-finite values.
Results may differ from the reference program's by a relative error of at most 0.017.
Values may be sent and summed in bfloat16 or wider, within the bound.
No kernel may reach another device: no remote copies, remote signals or barrier semaphores. Data moves between devices by JAX's collectives and lax.ppermute only.
A program may use at most 192 MiB of HBM per device.

```python
import math
import jax
import jax.numpy as jnp
import numpy as np
from jax import lax

D = 1024
HEADS = 16
HEAD_DIM = 64
FF = 4096
SEQ_LEN = 512
SEQS = 8


def draw_w_qkv(key, part):
    column_index = jnp.arange(3 * D)
    weights_drawn = jax.random.truncated_normal(key, -4.0, 4.0, (D, 3 * D), jnp.float32) / math.sqrt(D)
    weights_drawn = jnp.where(column_index[None, :] < D, weights_drawn * 2.0, weights_drawn)
    return weights_drawn.astype(jnp.bfloat16)


def with_spikes(entries, stream_key, source, target, parts, factor):
    owner, partner = [(jnp.arange(entries.shape[position]) // (entries.shape[position] // parts)).reshape([-1 if axis == position else 1 for axis in range(entries.ndim)]) for position in (source, target)]
    chosen = jax.random.permutation(stream_key, parts)[partner]
    strong = (owner == chosen) | (owner == (partner + parts // 2) % parts)
    return jnp.where(strong, factor * entries, entries)


def steps_of(rng, dims, shards, least, top_value):
    def one(axis_at, blocks):
        steps = jax.random.uniform(jax.random.fold_in(jax.random.fold_in(rng, 6), axis_at), (blocks,), jnp.float32, least / len(shards), top_value / len(shards))
        return jnp.repeat(jnp.exp(steps), dims[axis_at] // blocks).reshape((-1,) + (1,) * (len(dims) - axis_at - 1))

    level = one(*shards[0])
    for cut in shards[1:]:
        level = level * one(*cut)
    return level


def profile(number_of, total, bound, lean):
    portions = [(1 << 20) // math.isqrt(rank ** lean) + 1 for rank in range(2, number_of + 1)]
    surplus, counts = total - bound - (number_of - 1), [1] * (number_of - 1)
    while surplus > 0:
        movable = [i for i in range(number_of - 1) if counts[i] < bound]
        pool, remaining = sum([portions[i] for i in movable]), surplus
        for i in movable:
            extra = min(bound - counts[i], max(1, remaining * portions[i] // pool), surplus)
            counts[i] = counts[i] + extra
            surplus = surplus - extra
    return np.array([bound] + counts)


def uneven(own_key, amount, total, most, skew):
    if amount == 2:
        one = jax.random.randint(own_key, (), max(1, total - most), min(most, total - 1) + 1)
        return jnp.stack([one, total - one])
    tallies = jnp.asarray(profile(amount, total, most, skew), jnp.int32)
    twos = (amount - 1) // 2
    giver, receiver = tallies[1:1 + 2 * twos:2], tallies[2:2 + 2 * twos:2]
    room = jnp.minimum(giver - 1, most - receiver)
    passed = jax.random.randint(jax.random.fold_in(own_key, 1), (twos,), 0, 1 << 20) % (room + 1)
    tallies = tallies.at[1:1 + 2 * twos:2].set(giver - passed).at[2:2 + 2 * twos:2].set(receiver + passed)
    return tallies[jax.random.permutation(jax.random.fold_in(own_key, 2), amount)]


def centred(stream_key, dims, deviation, most, shards=(), held_as=jnp.bfloat16):
    level = steps_of(stream_key, dims, shards, -0.22, 0.18) if shards else 1.0
    drawn = jax.random.normal(stream_key, dims, jnp.float32) * deviation * level
    return jnp.minimum(jnp.maximum(drawn, -most), most).astype(held_as)


def noise_with(rng, extent, spread, most, pieces, heavy, held_as=jnp.bfloat16):
    drawn = spread * jax.random.normal(rng, extent, jnp.float32)
    if pieces:
        drawn = drawn * steps_of(rng, extent, pieces, -0.22, 0.18)
    return jnp.clip(with_spikes(drawn, jax.random.fold_in(rng, 3), *heavy), -most, most).astype(held_as)


def setup_inputs(seed: int = 0) -> dict:
    arg_keys = jax.random.split(jax.random.key(seed), 16)
    return {
        "layer_input": centred(arg_keys[0], (SEQS, SEQ_LEN, D), 1.0, 6.0, ((0, 8), (1, 4)), jnp.float32),
        "segment_ids": jax.vmap(lambda own: jnp.searchsorted(jnp.cumsum(uneven(own, 3, SEQ_LEN, 3 * SEQ_LEN // 4, 1)), jnp.arange(SEQ_LEN), side="right"))(jax.random.split(arg_keys[1], SEQS)).reshape((SEQS, SEQ_LEN)).astype(jnp.int32),
        "ln1_gain": jnp.clip(1.0 + 0.18 * jax.random.normal(arg_keys[2], (D,), jnp.float32), 0.1, 1.9),
        "ln1_bias": centred(arg_keys[3], (D,), 0.5, 3.0, (), jnp.float32),
        "w_qkv": draw_w_qkv(jax.random.fold_in(arg_keys[15], 71), 0),
        "qv_bias": centred(arg_keys[5], (2 * D,), 0.5, 3.0, (), jnp.float32),
        "w_out": centred(arg_keys[6], (D, D), (D // 16) ** -0.5, 0.75, ((0, 8), (1, 4))),
        "out_bias": centred(arg_keys[7], (D,), 0.5, 3.0, (), jnp.float32),
        "ln2_gain": jnp.clip(1.0 + 0.18 * jax.random.normal(arg_keys[8], (D,), jnp.float32), 0.1, 1.9),
        "ln2_bias": centred(arg_keys[9], (D,), 0.5, 3.0, (), jnp.float32),
        "w_up": centred(arg_keys[10], (D, FF), D ** -0.5, 0.1875, ((0, 8), (1, 4))),
        "up_bias": centred(arg_keys[11], (FF,), 0.5, 3.0, (), jnp.float32),
        "w_down": centred(arg_keys[12], (FF, D), FF ** -0.5, 0.09375, ((0, 8), (1, 4))),
        "down_bias": centred(arg_keys[13], (D,), 0.5, 3.0, (), jnp.float32),
        "cotangent": noise_with(arg_keys[14], (SEQS, SEQ_LEN, D), 1.0, 6.0, ((0, 8), (1, 4)), (1, 2, 4, 2.0), jnp.float32),
    }


epsilon = 1e-05
gelu_scale = 0.7978845608028654
cubic_term = 0.044715
neg_large = -1e+30

def layer_norm(values, gain, offset):
    center = lax.optimization_barrier(jnp.mean(values, axis=-1, keepdims=True))
    centered = values - center
    variance = lax.optimization_barrier(jnp.mean(centered * centered, axis=-1, keepdims=True))
    inv_std = lax.rsqrt(variance + epsilon)
    normed = centered * inv_std
    return (normed * gain + offset, normed, inv_std)

def norm_backward(upstream, normed, inv_std, gain):
    scaled = upstream * gain
    return inv_std * (scaled - lax.optimization_barrier(jnp.mean(scaled, axis=-1, keepdims=True)) - normed * lax.optimization_barrier(jnp.mean(scaled * normed, axis=-1, keepdims=True)))

def gelu_forward(values):
    inner = gelu_scale * (values + cubic_term * values * values * values)
    return 0.5 * values * (1.0 + jnp.tanh(inner))

def gelu_slope(values):
    tangent = jnp.tanh(gelu_scale * (values + cubic_term * values * values * values))
    return 0.5 * (1.0 + tangent) + 0.5 * values * (1.0 - tangent * tangent) * gelu_scale * (1.0 + 3.0 * cubic_term * values * values)

def alibi_slopes():
    return jnp.exp2(-8.0 * jnp.arange(1, HEADS + 1).astype(jnp.float32) / HEADS)

def reference(layer_input, segment_ids, ln1_gain, ln1_bias, w_qkv, qv_bias, w_out, out_bias, ln2_gain, ln2_bias, w_up, up_bias, w_down, down_bias, cotangent):
    slopes = alibi_slopes()
    inv_root = 1.0 / math.sqrt(HEAD_DIM)

    def one_sequence(totals, item):
        stream, seg_row, upstream = item
        seq_len = stream.shape[0]
        positions = jnp.arange(seq_len).astype(jnp.float32)
        allowed = (positions[None, :] <= positions[:, None]) & (seg_row[None, :] == seg_row[:, None])

        def split_heads(matrix):
            return matrix.reshape(seq_len, HEADS, HEAD_DIM).transpose(1, 0, 2)

        def merge_heads(tensor):
            return tensor.transpose(1, 0, 2).reshape(seq_len, D)

        def head_scores(query_head, key_head, slope):
            raw = jnp.dot(query_head, key_head.T, preferred_element_type=jnp.float32) * inv_root
            raw = raw - slope * (positions[:, None] - positions[None, :])
            return jnp.where(allowed, raw, neg_large)
        normed1_out, normed1, inv_std1 = layer_norm(stream, ln1_gain, ln1_bias)
        ln1_act = normed1_out.astype(jnp.bfloat16)
        projected = jnp.dot(ln1_act, w_qkv, preferred_element_type=jnp.float32)
        query = (projected[:, :D] + qv_bias[:D]).astype(jnp.bfloat16)
        keys = projected[:, D:2 * D].astype(jnp.bfloat16)
        values = (projected[:, 2 * D:] + qv_bias[D:]).astype(jnp.bfloat16)
        query_heads = split_heads(query)
        key_heads = split_heads(keys)
        value_heads = split_heads(values)

        def head_forward(head_item):
            query_head, key_head, value_head, slope = head_item
            scores = head_scores(query_head, key_head, slope)
            row_max = lax.optimization_barrier(jnp.max(scores, axis=-1))
            probs_raw = jnp.where(allowed, jnp.exp(scores - row_max[:, None]), 0.0)
            row_sum = lax.optimization_barrier(jnp.sum(probs_raw, axis=-1))
            output = jnp.dot(probs_raw.astype(jnp.bfloat16), value_head, preferred_element_type=jnp.float32) / row_sum[:, None]
            return (output, row_max + jnp.log(row_sum))
        head_out, log_sum = lax.map(head_forward, (query_heads, key_heads, value_heads, slopes))
        attn = merge_heads(head_out).astype(jnp.bfloat16)
        middle = stream + jnp.dot(attn, w_out, preferred_element_type=jnp.float32) + out_bias
        normed2_out, normed2, inv_std2 = layer_norm(middle, ln2_gain, ln2_bias)
        ln2_act = normed2_out.astype(jnp.bfloat16)
        pre_act = jnp.dot(ln2_act, w_up, preferred_element_type=jnp.float32) + up_bias
        hidden = gelu_forward(pre_act).astype(jnp.bfloat16)
        result = middle + jnp.dot(hidden, w_down, preferred_element_type=jnp.float32) + down_bias
        cot_bf = upstream.astype(jnp.bfloat16)
        grad_down = jnp.dot(hidden.T, cot_bf, preferred_element_type=jnp.float32)
        down_bias_grad = lax.optimization_barrier(jnp.sum(upstream, axis=0))
        pre_grad = jnp.dot(cot_bf, w_down.T, preferred_element_type=jnp.float32) * gelu_slope(pre_act)
        pre_bf = pre_grad.astype(jnp.bfloat16)
        grad_up = jnp.dot(ln2_act.T, pre_bf, preferred_element_type=jnp.float32)
        up_bias_grad = lax.optimization_barrier(jnp.sum(pre_grad, axis=0))
        ln2_out_grad = jnp.dot(pre_bf, w_up.T, preferred_element_type=jnp.float32)
        ln2_gain_grad = lax.optimization_barrier(jnp.sum(ln2_out_grad * normed2, axis=0))
        ln2_bias_grad = lax.optimization_barrier(jnp.sum(ln2_out_grad, axis=0))
        middle_grad = upstream + norm_backward(ln2_out_grad, normed2, inv_std2, ln2_gain)
        middle_bf = middle_grad.astype(jnp.bfloat16)
        grad_out = jnp.dot(attn.T, middle_bf, preferred_element_type=jnp.float32)
        out_bias_grad = lax.optimization_barrier(jnp.sum(middle_grad, axis=0))
        attn_grad = jnp.dot(middle_bf, w_out.T, preferred_element_type=jnp.float32).astype(jnp.bfloat16)
        row_delta = lax.optimization_barrier(jnp.sum((attn_grad.astype(jnp.float32) * attn.astype(jnp.float32)).reshape(seq_len, HEADS, HEAD_DIM), axis=-1)).T
        grad_heads = split_heads(attn_grad)

        def head_backward(head_item):
            query_head, key_head, value_head, slope, head_lse, head_grad, head_delta = head_item
            scores = head_scores(query_head, key_head, slope)
            probs = jnp.where(allowed, jnp.exp(scores - head_lse[:, None]), 0.0)
            prob_grad = jnp.dot(head_grad, value_head.T, preferred_element_type=jnp.float32)
            score_grad = probs * (prob_grad - head_delta[:, None])
            probs_bf = probs.astype(jnp.bfloat16)
            score_bf = score_grad.astype(jnp.bfloat16)
            query_grad = inv_root * jnp.dot(score_bf, key_head, preferred_element_type=jnp.float32)
            key_grad = inv_root * jnp.dot(score_bf.T, query_head, preferred_element_type=jnp.float32)
            value_grad = jnp.dot(probs_bf.T, head_grad, preferred_element_type=jnp.float32)
            return (query_grad, key_grad, value_grad)
        query_grad, key_grad, value_grad = lax.map(head_backward, (query_heads, key_heads, value_heads, slopes, log_sum, grad_heads, row_delta))
        query_flat = merge_heads(query_grad)
        value_flat = merge_heads(value_grad)
        qkv_bf = jnp.concatenate([query_flat, merge_heads(key_grad), value_flat], axis=1).astype(jnp.bfloat16)
        grad_qkv = jnp.dot(ln1_act.T, qkv_bf, preferred_element_type=jnp.float32)
        qv_bias_grad = jnp.concatenate([lax.optimization_barrier(jnp.sum(query_flat, axis=0)), lax.optimization_barrier(jnp.sum(value_flat, axis=0))])
        ln1_out_grad = jnp.dot(qkv_bf, w_qkv.T, preferred_element_type=jnp.float32)
        ln1_gain_grad = lax.optimization_barrier(jnp.sum(ln1_out_grad * normed1, axis=0))
        ln1_bias_grad = lax.optimization_barrier(jnp.sum(ln1_out_grad, axis=0))
        input_grad = middle_grad + norm_backward(ln1_out_grad, normed1, inv_std1, ln1_gain)
        terms = (ln1_gain_grad, ln1_bias_grad, grad_qkv, qv_bias_grad, grad_out, out_bias_grad, ln2_gain_grad, ln2_bias_grad, grad_up, up_bias_grad, grad_down, down_bias_grad)
        totals = tuple((total + term for total, term in zip(totals, terms)))
        return (totals, (result, input_grad))
    zeros_init = (jnp.zeros((D,), jnp.float32), jnp.zeros((D,), jnp.float32), jnp.zeros((D, 3 * D), jnp.float32), jnp.zeros((2 * D,), jnp.float32), jnp.zeros((D, D), jnp.float32), jnp.zeros((D,), jnp.float32), jnp.zeros((D,), jnp.float32), jnp.zeros((D,), jnp.float32), jnp.zeros((D, FF), jnp.float32), jnp.zeros((FF,), jnp.float32), jnp.zeros((FF, D), jnp.float32), jnp.zeros((D,), jnp.float32))
    totals, outputs = lax.scan(one_sequence, zeros_init, (layer_input, segment_ids, cotangent))
    result, input_grad = outputs
    return (result, input_grad, totals[0], totals[1], totals[2], totals[3], totals[4], totals[5], totals[6], totals[7], totals[8], totals[9], totals[10], totals[11])
```

```python
import math

import jax
import jax.numpy as jnp
from jax import lax
from jax.experimental import pallas as pl
from jax.experimental.pallas import tpu as pltpu
from jax.sharding import PartitionSpec as P

HEADS = 16
HEAD_DIM = 64

epsilon = 1e-05
gelu_scale = 0.7978845608028654
cubic_term = 0.044715
neg_large = -1e30
BF = jnp.bfloat16
F32 = jnp.float32


def layer_norm(values, gain, offset):
    center = jnp.mean(values, axis=-1, keepdims=True)
    centered = values - center
    variance = jnp.mean(centered * centered, axis=-1, keepdims=True)
    inv_std = lax.rsqrt(variance + epsilon)
    normed = centered * inv_std
    return (normed * gain + offset, normed, inv_std)


def norm_backward(upstream, normed, inv_std, gain):
    scaled = upstream * gain
    return inv_std * (
        scaled
        - jnp.mean(scaled, axis=-1, keepdims=True)
        - normed * jnp.mean(scaled * normed, axis=-1, keepdims=True)
    )


def gelu_both(values):
    square = values * values
    tangent = jnp.tanh(gelu_scale * (values + cubic_term * values * square))
    forward = 0.5 * values * (1.0 + tangent)
    slope = 0.5 * (1.0 + tangent) + 0.5 * values * (1.0 - tangent * tangent) * gelu_scale * (
        1.0 + 3.0 * cubic_term * square
    )
    return forward, slope


def dot(a, b):
    return jnp.dot(a, b, preferred_element_type=F32)


def dot_nt(a, b):
    return lax.dot_general(a, b, (((1,), (1,)), ((), ())), preferred_element_type=F32)


def dot_tn(a, b):
    return lax.dot_general(a, b, (((0,), (0,)), ((), ())), preferred_element_type=F32)


def pick(stack, index):
    return lax.dynamic_index_in_dim(stack, index, 0, keepdims=False)


def ctx_bits(count):
    bits = []
    bit = count // 2
    while bit:
        bits.append(bit)
        bit //= 2
    return bits


def ctx_order(count):
    order = [0]
    for bit in ctx_bits(count):
        order = order + [r | bit for r in order]
    return order


def ctx_swap(x, bit):
    count = lax.axis_size("ctx")
    return lax.ppermute(x, "ctx", [(i, i ^ bit) for i in range(count)])


def ctx_gather(x):
    pieces = [x]
    for bit in ctx_bits(lax.axis_size("ctx")):
        pieces = pieces + [ctx_swap(p, bit) for p in pieces]
    return jnp.concatenate(pieces, axis=0)


def ctx_scatter(x):
    for bit in reversed(ctx_bits(lax.axis_size("ctx"))):
        half = x.shape[0] // 2
        x = x[:half] + ctx_swap(x[half:].astype(BF), bit).astype(F32)
    return x


def ctx_exchange(pieces):
    pieces = list(pieces)
    for bit in ctx_bits(lax.axis_size("ctx")):
        slots = [r for r in range(len(pieces)) if r & bit]
        got = ctx_swap(jnp.stack([pieces[r] for r in slots]), bit)
        for i, r in enumerate(slots):
            pieces[r] = got[i]
    return pieces


def by_owner(pieces, me, axis):
    stack = jnp.stack(pieces)
    return jnp.concatenate([pick(stack, me ^ k) for k in range(len(pieces))], axis=axis)


def dp_shape(count):
    z_count = 4 if count % 4 == 0 else count
    return z_count, count // z_count


def ring_z(x):
    count = lax.axis_size("dp")
    _, y_count = dp_shape(count)
    return lax.ppermute(x, "dp", [(i, (i + y_count) % count) for i in range(count)])


def ring_y(x):
    count = lax.axis_size("dp")
    _, y_count = dp_shape(count)
    return lax.ppermute(
        x, "dp", [(i, i // y_count * y_count + (i + 1) % y_count) for i in range(count)]
    )


def dp_blocks(x):
    z_count, y_count = dp_shape(lax.axis_size("dp"))
    blocks = []
    for s in range(z_count):
        moving = x
        blocks.append(moving)
        for _ in range(y_count - 1):
            moving = ring_y(moving)
            blocks.append(moving)
        if s < z_count - 1:
            x = ring_z(x)
    return blocks


def dp_places(reverse=False):
    count = lax.axis_size("dp")
    z_count, y_count = dp_shape(count)
    me = lax.axis_index("dp")
    z, y = me // y_count, me % y_count
    places = []
    for s in range(z_count):
        for t in range(y_count):
            places.append((z + z_count - s) % z_count * y_count + (y + y_count - t) % y_count)
    return places


def assemble(blocks, places, widths):
    count = len(blocks)
    rows = blocks[0].shape[0]
    outs = len(widths)

    def kernel(*refs):
        place_ref, in_refs, out_refs = refs[0], refs[1 : 1 + count], refs[1 + count :]
        for i in range(count):
            at = pl.multiple_of(place_ref[i] * rows, rows)
            start = 0
            for out_ref, w in zip(out_refs, widths):
                out_ref[pl.ds(at, rows), :] = in_refs[i][:, start : start + w]
                start += w

    return pl.pallas_call(
        kernel,
        out_shape=[jax.ShapeDtypeStruct((rows * count, w), blocks[0].dtype) for w in widths],
        in_specs=[pl.BlockSpec(memory_space=pltpu.SMEM)]
        + [pl.BlockSpec(memory_space=pltpu.VMEM)] * count,
        out_specs=[pl.BlockSpec(memory_space=pltpu.VMEM)] * outs,
        compiler_params=pltpu.CompilerParams(vmem_limit_bytes=32 * 2**20),
    )(jnp.stack(places).astype(jnp.int32), *blocks)


def dp_reduce(block_of):
    z_count, y_count = dp_shape(lax.axis_size("dp"))
    total = None
    for s in list(range(1, z_count)) + [0]:
        part = None
        for t in list(range(1, y_count)) + [0]:
            mine = block_of(s, t)
            part = mine if part is None else mine.astype(F32) + part
            if t:
                part = ring_y(part.astype(BF)).astype(F32)
        part = part.astype(F32)
        total = part if total is None else total + part
        if s:
            total = ring_z(total.astype(BF)).astype(F32)
    return total


def all_sum(x):
    for bit in reversed(ctx_bits(lax.axis_size("ctx"))):
        x = x + ctx_swap(x, bit)
    count = lax.axis_size("dp")
    bit = 1
    while bit < count:
        x = x + lax.ppermute(x, "dp", [(i, i ^ bit) for i in range(count)])
        bit *= 2
    return x


def per_device(
    layer_input,
    segment_ids,
    ln1_gain,
    ln1_bias,
    w_qkv,
    qv_bias,
    w_out,
    out_bias,
    ln2_gain,
    ln2_bias,
    w_up,
    up_bias,
    w_down,
    down_bias,
    cotangent,
):
    stream = layer_input[0]
    upstream = cotangent[0]
    seg_row = segment_ids[0]
    rows, width = stream.shape
    ctx = lax.axis_size("ctx")
    dps = lax.axis_size("dp")
    c = lax.axis_index("ctx")
    seq = rows * ctx
    unit = width // ctx
    heads = HEADS // ctx
    inv_root = 1.0 / math.sqrt(HEAD_DIM)
    ff = up_bias.shape[0]
    sub = ff // dps // ctx
    order = ctx_order(ctx)
    slots = [order.index(r) for r in range(ctx)]
    places = dp_places()

    took = [
        lax.ppermute(
            w_qkv[:, j * unit : (j + 1) * unit], "ctx", [(i, (3 * i + j) % ctx) for i in range(ctx)]
        )
        for j in range(3)
    ]
    took = jnp.stack(took)
    head_qkv = jnp.concatenate([pick(took, (kind * ctx + c) % 3) for kind in range(3)], axis=1)
    qkv_blocks = dp_blocks(head_qkv)

    normed1_out, normed1, inv_std1 = layer_norm(stream, ln1_gain, ln1_bias)
    ln1_act = normed1_out.astype(BF)
    ln1_all = ctx_gather(ln1_act)
    cot_all = ctx_gather(upstream.astype(BF))

    out_blocks = dp_blocks(w_out)
    down_view = w_down.reshape(ctx, sub, unit)
    up_view = jnp.moveaxis(w_up.reshape(w_up.shape[0], dps // ctx, ctx, sub), 2, 0).reshape(
        ctx, sub, unit
    )
    pieces = ctx_exchange(
        [jnp.stack([pick(up_view, c ^ r), pick(down_view, c ^ r)]) for r in range(ctx)]
    )
    unit_up = by_owner([p[0].reshape(w_up.shape[0], -1) for p in pieces], c, 1)
    unit_down = by_owner([p[1] for p in pieces], c, 1)
    up_blocks = dp_blocks(unit_up)
    down_blocks = dp_blocks(unit_down)

    (full_qkv,) = assemble(qkv_blocks, places, [3 * unit])
    (col_out,) = assemble(out_blocks, places, [unit])
    out_gathered = ctx_gather(col_out).reshape(ctx, width, unit)
    full_out = jnp.concatenate([pick(out_gathered, jnp.asarray(slots)[c ^ k]) for k in range(ctx)], axis=1)
    (full_up,) = assemble(up_blocks, places, [dps * sub])
    (full_down,) = assemble(down_blocks, places, [width])

    projected = dot(ln1_all, full_qkv)
    q_bias = lax.dynamic_slice_in_dim(qv_bias, c * unit, unit)
    v_bias = lax.dynamic_slice_in_dim(qv_bias, width + c * unit, unit)
    query = (projected[:, :unit] + q_bias).astype(BF)
    keys = projected[:, unit : 2 * unit].astype(BF)
    values = (projected[:, 2 * unit :] + v_bias).astype(BF)

    seg_blocks = seg_row.reshape(ctx, rows)
    seg = jnp.concatenate([pick(seg_blocks, c ^ r) for r in order])
    pos = jnp.concatenate([(c ^ r) * rows + jnp.arange(rows, dtype=jnp.int32) for r in order])
    pos_f = pos.astype(F32)
    allowed = (pos[None, :] <= pos[:, None]) & (seg[None, :] == seg[:, None])
    head_ids = (c * heads + 1 + jnp.arange(heads)).astype(F32)
    slopes = jnp.exp2(-8.0 * head_ids / HEADS)

    def split(x):
        return x.reshape(seq, heads, HEAD_DIM)

    query3, keys3, values3 = split(query), split(keys), split(values)
    raw = jnp.einsum("chd,nhd->hcn", query3, keys3, preferred_element_type=F32)
    raw = raw * inv_root - slopes[:, None, None] * (pos_f[None, :, None] - pos_f[None, None, :])
    scores = jnp.where(allowed[None], raw, neg_large)
    row_max = jnp.max(scores, axis=-1, keepdims=True)
    probs_raw = jnp.where(allowed[None], jnp.exp(scores - row_max), 0.0)
    row_sum = jnp.sum(probs_raw, axis=-1, keepdims=True)
    head_out = (
        jnp.einsum("hcn,nhd->hcd", probs_raw.astype(BF), values3, preferred_element_type=F32)
        / row_sum
    )
    log_sum = row_max + jnp.log(row_sum)
    attn_heads = head_out.transpose(1, 0, 2).reshape(seq, unit).astype(BF)

    def to_tokens(x):
        view = x.reshape(ctx, rows, unit)
        return by_owner(ctx_exchange([view[slots[r]] for r in range(ctx)]), c, 1)

    def to_heads(x):
        view = jnp.stack([x[:, k * unit : (k + 1) * unit] for k in range(ctx)])
        got = ctx_exchange([pick(view, c ^ r) for r in range(ctx)])
        return jnp.concatenate([got[r] for r in order], axis=0)

    attn = to_tokens(attn_heads)
    middle = stream + dot(attn, full_out) + out_bias
    normed2_out, normed2, inv_std2 = layer_norm(middle, ln2_gain, ln2_bias)
    ln2_act = normed2_out.astype(BF)
    ln2_all = ctx_gather(ln2_act)
    unit_bias = pick(jnp.moveaxis(up_bias.reshape(dps, ctx, sub), 1, 0), c).reshape(dps * sub)
    pre_act = dot(ln2_all, full_up) + unit_bias
    hidden_f, slope_f = gelu_both(pre_act)
    hidden = hidden_f.astype(BF)
    pre_grad = dot_nt(cot_all, full_down) * slope_f
    pre_bf = pre_grad.astype(BF)
    ln2_out_grad = ctx_scatter(dot_nt(pre_bf, full_up))
    up_bias_part = jnp.sum(pre_grad, axis=0)

    middle_grad = upstream + norm_backward(ln2_out_grad, normed2, inv_std2, ln2_gain)
    middle_bf = middle_grad.astype(BF)
    attn_grad = to_heads(dot_nt(middle_bf, full_out).astype(BF))

    grad_down = dot_tn(hidden, cot_all).astype(BF).reshape(dps, sub, width)
    grad_up = dot_tn(ln2_all, pre_bf).astype(BF).reshape(dps, width // dps, dps * sub)
    y_count = dp_shape(dps)[1]

    def reduce_rows(grad):
        return dp_reduce(lambda s, t: pick(grad, places[s * y_count + t]))

    sum_down = reduce_rows(grad_down)
    sum_up = reduce_rows(grad_up)
    result = middle + ctx_scatter(dot(hidden, full_down)) + down_bias

    attn_all = ctx_gather(attn)
    middle_cols = to_heads(middle_bf)
    grad_out = dot_tn(attn_all, middle_cols).astype(BF).reshape(dps, width // dps, unit)
    sum_out = reduce_rows(grad_out)

    attn_grad3 = split(attn_grad)
    row_delta = jnp.sum(
        (attn_grad.astype(F32) * attn_heads.astype(F32)).reshape(seq, heads, HEAD_DIM), axis=-1
    ).T[..., None]
    probs = jnp.where(allowed[None], jnp.exp(scores - log_sum), 0.0)
    prob_grad = jnp.einsum("chd,nhd->hcn", attn_grad3, values3, preferred_element_type=F32)
    score_bf = (probs * (prob_grad - row_delta)).astype(BF)
    probs_bf = probs.astype(BF)

    def join(x):
        return x.reshape(seq, unit)

    query_grad = join(
        inv_root * jnp.einsum("hcn,nhd->chd", score_bf, keys3, preferred_element_type=F32)
    )
    key_grad = join(
        inv_root * jnp.einsum("hcn,chd->nhd", score_bf, query3, preferred_element_type=F32)
    )
    value_grad = join(
        jnp.einsum("hcn,chd->nhd", probs_bf, attn_grad3, preferred_element_type=F32)
    )
    qkv_bf = jnp.concatenate([query_grad, key_grad, value_grad], axis=1).astype(BF)
    ln1_out_grad = ctx_scatter(dot_nt(qkv_bf, full_qkv))
    grad_qkv = dot_tn(ln1_all, qkv_bf).astype(BF).reshape(dps, width // dps, 3 * unit)
    sum_qkv = reduce_rows(grad_qkv)
    input_grad = middle_grad + norm_backward(ln1_out_grad, normed1, inv_std1, ln1_gain)

    here = (jnp.arange(ctx) == c).astype(F32)
    q_part = (here[:, None] * jnp.sum(query_grad, axis=0)[None, :]).reshape(width)
    v_part = (here[:, None] * jnp.sum(value_grad, axis=0)[None, :]).reshape(width)
    up_part = (here[None, :, None] * up_bias_part.reshape(dps, 1, sub)).reshape(ff)
    early = jnp.concatenate(
        [
            jnp.sum(upstream, axis=0),
            up_part,
            jnp.sum(ln2_out_grad * normed2, axis=0),
            jnp.sum(ln2_out_grad, axis=0),
            jnp.sum(middle_grad, axis=0),
        ]
    )
    late = jnp.concatenate(
        [jnp.sum(ln1_out_grad * normed1, axis=0), jnp.sum(ln1_out_grad, axis=0), q_part, v_part]
    )
    early = all_sum(early.reshape(-1, 128)).reshape(-1)
    late = all_sum(late.reshape(-1, 128)).reshape(-1)
    down_bias_grad = early[:width]
    up_bias_grad = early[width : width + ff]
    ln2_gain_grad = early[width + ff : 2 * width + ff]
    ln2_bias_grad = early[2 * width + ff : 3 * width + ff]
    out_bias_grad = early[3 * width + ff :]

    kinds = jnp.stack([sum_qkv[:, k * unit : (k + 1) * unit] for k in range(3)]).astype(BF)
    shard_qkv = jnp.concatenate(
        [
            lax.ppermute(
                pick(kinds, ((j + 3 * ctx - c) * ctx) % 3),
                "ctx",
                [((3 * i + j) % ctx, i) for i in range(ctx)],
            )
            for j in range(3)
        ],
        axis=1,
    ).astype(F32)
    down_cols = jnp.moveaxis(sum_down.astype(BF).reshape(sub, ctx, unit), 1, 0)
    up_cols = jnp.moveaxis(sum_up.astype(BF).reshape(w_up.shape[0], ctx, -1), 1, 0).reshape(
        ctx, sub, unit
    )
    back = ctx_exchange(
        [jnp.stack([pick(up_cols, c ^ r), pick(down_cols, c ^ r)]) for r in range(ctx)]
    )
    shard_down = by_owner([p[1] for p in back], c, 0).astype(F32)
    shard_up = (
        by_owner([p[0].reshape(w_up.shape[0], dps // ctx, 1, sub) for p in back], c, 2)
        .reshape(w_up.shape)
        .astype(F32)
    )

    return (
        result[None],
        input_grad[None],
        late[:width],
        late[width : 2 * width],
        shard_qkv,
        late[2 * width :],
        sum_out,
        out_bias_grad,
        ln2_gain_grad,
        ln2_bias_grad,
        shard_up,
        up_bias_grad,
        shard_down,
        down_bias_grad,
    )


def solution(mesh):
    tokens = P("dp", "ctx", None)
    weight = P("dp", "ctx")
    placed = (
        tokens,
        P("dp", None),
        P(),
        P(),
        weight,
        P(),
        weight,
        P(),
        P(),
        P(),
        weight,
        P(),
        weight,
        P(),
        tokens,
    )
    return jax.shard_map(
        per_device,
        mesh=mesh,
        in_specs=placed,
        out_specs=(
            tokens,
            tokens,
            P(),
            P(),
            weight,
            P(),
            weight,
            P(),
            P(),
            P(),
            weight,
            P(),
            weight,
            P(),
        ),
        check_vma=False,
    )
```

```python
import math

import jax
import jax.numpy as jnp
from jax import lax
from jax.experimental import pallas as pl
from jax.experimental.pallas import tpu as pltpu
from jax.sharding import PartitionSpec as P

HEADS = 16
HEAD_DIM = 64

epsilon = 1e-05
gelu_scale = 0.7978845608028654
cubic_term = 0.044715
neg_large = -1e30
BF = jnp.bfloat16
F32 = jnp.float32


def layer_norm(values, gain, offset):
    center = jnp.mean(values, axis=-1, keepdims=True)
    centered = values - center
    variance = jnp.mean(centered * centered, axis=-1, keepdims=True)
    inv_std = lax.rsqrt(variance + epsilon)
    normed = centered * inv_std
    return (normed * gain + offset, normed, inv_std)


def norm_backward(upstream, normed, inv_std, gain):
    scaled = upstream * gain
    return inv_std * (
        scaled
        - jnp.mean(scaled, axis=-1, keepdims=True)
        - normed * jnp.mean(scaled * normed, axis=-1, keepdims=True)
    )


def gelu_both(values):
    square = values * values
    tangent = jnp.tanh(gelu_scale * (values + cubic_term * values * square))
    forward = 0.5 * values * (1.0 + tangent)
    slope = 0.5 * (1.0 + tangent) + 0.5 * values * (1.0 - tangent * tangent) * gelu_scale * (
        1.0 + 3.0 * cubic_term * square
    )
    return forward, slope


def dot(a, b):
    return jnp.dot(a, b, preferred_element_type=F32)


def dot_nt(a, b):
    return lax.dot_general(a, b, (((1,), (1,)), ((), ())), preferred_element_type=F32)


def dot_tn(a, b):
    return lax.dot_general(a, b, (((0,), (0,)), ((), ())), preferred_element_type=F32)


def pick(stack, index):
    return lax.dynamic_index_in_dim(stack, index, 0, keepdims=False)


def ctx_bits(count):
    bits = []
    bit = count // 2
    while bit:
        bits.append(bit)
        bit //= 2
    return bits


def ctx_order(count):
    order = [0]
    for bit in ctx_bits(count):
        order = order + [r | bit for r in order]
    return order


def ctx_swap(x, bit):
    count = lax.axis_size("ctx")
    return lax.ppermute(x, "ctx", [(i, i ^ bit) for i in range(count)])


def gather_step(pieces, bit):
    return pieces + [ctx_swap(p, bit) for p in pieces]


def ctx_gather(x):
    pieces = [x]
    for bit in ctx_bits(lax.axis_size("ctx")):
        pieces = gather_step(pieces, bit)
    return jnp.concatenate(pieces, axis=0)


def ctx_scatter(x):
    for bit in reversed(ctx_bits(lax.axis_size("ctx"))):
        half = x.shape[0] // 2
        x = x[:half] + ctx_swap(x[half:].astype(BF), bit).astype(F32)
    return x


def exchange_step(pieces, bit):
    pieces = list(pieces)
    slots = [r for r in range(len(pieces)) if r & bit]
    got = ctx_swap(jnp.stack([pieces[r] for r in slots]), bit)
    for i, r in enumerate(slots):
        pieces[r] = got[i]
    return pieces


def ctx_exchange(pieces):
    for bit in ctx_bits(lax.axis_size("ctx")):
        pieces = exchange_step(pieces, bit)
    return pieces


def trade(near, far):
    count = 2 * near.shape[0]
    if count == 4:
        got = ctx_swap(far, 2)
        return [(near, 0), (ctx_swap(near, 1), 1), (got, 0), (ctx_swap(got, 1), 1)]
    pieces = ctx_exchange([*near, *far])
    return [(piece[None], 0) for piece in pieces]


def put_piece(near_ref, far_ref, r, value):
    half = near_ref.shape[0]
    (near_ref if r < half else far_ref)[r % half] = value


def put_piece_at(near_ref, far_ref, slot, value):
    half = near_ref.shape[0]

    @pl.when(slot < half)
    def _():
        near_ref[slot] = value

    @pl.when(slot >= half)
    def _():
        far_ref[slot - half] = value


def piece_shapes(ctx, rows, width):
    return [((ctx // 2, rows, width), BF)] * 2


def owned(ids, pieces, k):
    value = pieces[0]
    for r in range(1, len(pieces)):
        value = jnp.where(ids[0] == (k ^ r), pieces[r], value)
    return value


def by_owner(pieces, me, axis):
    stack = jnp.stack(pieces)
    return jnp.concatenate([pick(stack, me ^ k) for k in range(len(pieces))], axis=axis)


def dp_shape(count):
    z_count = 4 if count % 4 == 0 else count
    return z_count, count // z_count


def ring_z(x):
    count = lax.axis_size("dp")
    _, y_count = dp_shape(count)
    return lax.ppermute(x, "dp", [(i, (i + y_count) % count) for i in range(count)])


def ring_y(x):
    count = lax.axis_size("dp")
    _, y_count = dp_shape(count)
    return lax.ppermute(
        x, "dp", [(i, i // y_count * y_count + (i + 1) % y_count) for i in range(count)]
    )


def along_y(x):
    row = [x]
    for _ in range(dp_shape(lax.axis_size("dp"))[1] - 1):
        row.append(ring_y(row[-1]))
    return row


def dp_places(reverse=False):
    count = lax.axis_size("dp")
    z_count, y_count = dp_shape(count)
    me = lax.axis_index("dp")
    z, y = me // y_count, me % y_count
    places = []
    for s in range(z_count):
        for t in range(y_count):
            places.append((z + z_count - s) % z_count * y_count + (y + y_count - t) % y_count)
    return places


def after(x, *earlier):
    return lax.optimization_barrier((x, *earlier))[0]


def call(kernel, outs, args, scalars=1, scratch=(), work=0, earlier=(), far=()):
    used = len(args)
    sizes = [(x.shape, x.dtype) for x in args] + list(outs) + [(x.shape, x.dtype) for x in scratch]
    held = sum(math.prod(shape) * jnp.dtype(dtype).itemsize for shape, dtype in sizes)
    limit = held * 5 // 4 + work + 4 * 2**20
    first_out = used + len(earlier)
    fetched = [pltpu.VMEM(args[i].shape, args[i].dtype) for i in far]
    if far:
        fetched.append(pltpu.SemaphoreType.DMA((len(far),)))

    def body(*refs):
        ins, rest = list(refs[:used]), refs[first_out:]
        if far:
            rest, buffers, sem = rest[: -len(far) - 1], rest[-len(far) - 1 : -1], rest[-1]
            copies = [
                pltpu.make_async_copy(ins[i], buffer, sem.at[j])
                for j, (i, buffer) in enumerate(zip(far, buffers))
            ]
            for copy in copies:
                copy.start()
            for copy in copies:
                copy.wait()
            for i, buffer in zip(far, buffers):
                ins[i] = buffer
        kernel(*ins, *rest)

    def space(i):
        if i in far:
            return pltpu.HBM
        return pltpu.SMEM if i < scalars else pl.ANY if i >= used else pltpu.VMEM

    return pl.pallas_call(
        body,
        out_shape=[jax.ShapeDtypeStruct(shape, dtype) for shape, dtype in outs],
        in_specs=[pl.BlockSpec(memory_space=space(i)) for i in range(first_out)],
        out_specs=[pl.BlockSpec(memory_space=pltpu.VMEM)] * len(outs),
        scratch_shapes=[*scratch, *fetched],
        compiler_params=pltpu.CompilerParams(vmem_limit_bytes=limit),
    )(*args, *earlier)


def assemble(full, blocks, places, cuts):
    count, held = len(blocks), len(cuts)
    shapes = [cut(jnp.zeros(blocks[0].shape, BF)).shape for cut in cuts]
    total = lax.axis_size("dp")

    def kernel(place_ref, *refs):
        outs = refs[-held:]
        for i in range(count):
            for out_ref, cut, (rows, _) in zip(outs, cuts, shapes):
                at = pl.multiple_of(place_ref[i] * rows, rows)
                out_ref[pl.ds(at, rows), :] = cut(refs[i])

    return pl.pallas_call(
        kernel,
        out_shape=[jax.ShapeDtypeStruct((total * rows, width), BF) for rows, width in shapes],
        in_specs=[pl.BlockSpec(memory_space=pltpu.SMEM)]
        + [pl.BlockSpec(memory_space=pltpu.VMEM)] * (count + (held if full else 0)),
        out_specs=[pl.BlockSpec(memory_space=pltpu.VMEM)] * held,
        input_output_aliases={1 + count + j: j for j in range(held)} if full else {},
        compiler_params=pltpu.CompilerParams(
            vmem_limit_bytes=4 * 2**20 + 6 * sum(total * rows * width for rows, width in shapes)
        ),
    )(jnp.stack(places).astype(jnp.int32), *blocks, *(full or []))


def dp_bits():
    bits = []
    bit = 1
    while bit < lax.axis_size("dp"):
        bits.append(bit)
        bit *= 2
    return bits


def slot_order(bits):
    order = [0]
    for bit in reversed(bits):
        order = order + [r | bit for r in order]
    return order


def grad_blocks(ids, left_ref, right, keep_ref, *send_refs):
    half, rows = keep_ref.shape[:2]
    bits = []
    while 2 ** len(bits) < 2 * half:
        bits.append(2 ** len(bits))
    ranges = [(keep_ref, 0)]
    for ref in send_refs[::-1]:
        ranges.append((ref, ranges[-1][1] + ranges[-1][0].shape[0]))
    for k in range(2 * half):
        block = dot_tn(left_ref[:, k * rows : (k + 1) * rows], right).astype(BF)
        name = jnp.bitwise_xor(ids[1], k)
        slot = 0
        for i, bit in enumerate(bits):
            slot = slot + lax.div(jnp.bitwise_and(name, bit), bit) * (half >> i)
        for ref, first in ranges:

            @pl.when((slot >= first) & (slot < first + ref.shape[0]))
            def _():
                ref[slot - first] = block


def block_shapes(dps, rows, width, parts):
    half = dps // 2
    counts = [half] + ([half] if parts == 1 else [half - half // 2, half // 2])
    return [((n, rows, width), BF) for n in counts]


def dp_swap(x, bit):
    count = lax.axis_size("dp")
    return lax.ppermute(x, "dp", [(i, i ^ bit) for i in range(count)])


def combine(terms, start, count, outs, write, earlier=()):

    def kernel(ids, *refs):
        for i in range(count):
            total = refs[0][start - terms[0][1] + i].astype(F32)
            for ref, (_, first) in zip(refs[1 : len(terms)], terms[1:]):
                total = total + ref[start - first + i].astype(F32)
            write(ids, i, total, refs[len(terms) :])

    ids = lax.axis_index("ctx").astype(jnp.int32)[None]
    return call(kernel, outs, [ids] + [array for array, _ in terms], earlier=earlier)


class Reduction:

    def __init__(self, blocks):
        keep, *sends = blocks
        self.bits = dp_bits()
        self.size = keep.shape[0]
        bit = self.bits.pop(0)
        got = [dp_swap(send, bit) for send in sends]
        self.first = [(keep, 0), (got[0], self.size - got[0].shape[0])]
        self.terms = [(keep, 0), (got[-1], 0)]

    def step(self, *earlier):
        self.size //= 2
        terms, self.first = self.first or self.terms, None

        def write(ids, i, block, refs):
            refs[0][i] = block.astype(BF)

        shape = (self.size,) + terms[0][0].shape[1:]
        (send,) = combine(terms, self.size, self.size, [(shape, BF)], write, earlier)
        self.terms.append((dp_swap(send, self.bits.pop(0)), 0))
        return send

    def result(self, outs, write, *earlier):
        return combine(self.terms, 0, 1, outs, write, earlier)


def sync(reductions, *values):
    held = [([a for a, _ in r.first or []], [a for a, _ in r.terms]) for r in reductions]
    held, values = lax.optimization_barrier((held, values))
    for r, (first, terms) in zip(reductions, held):
        if r.first:
            r.first = [(a, at) for a, (_, at) in zip(first, r.first)]
        r.terms = [(a, at) for a, (_, at) in zip(terms, r.terms)]
    return values


def unit_pieces(w_up, w_down, c, sub, unit):
    ctx, dps = lax.axis_size("ctx"), lax.axis_size("dp")
    down_view = w_down.reshape(ctx, sub, unit)
    up_view = jnp.moveaxis(w_up.reshape(w_up.shape[0], dps // ctx, ctx, sub), 2, 0).reshape(
        ctx, sub, unit
    )
    return [jnp.stack([pick(up_view, c ^ r), pick(down_view, c ^ r)]) for r in range(ctx)]


def join_units(pieces, c, up_rows):
    unit_up = by_owner([p[0].reshape(up_rows, -1) for p in pieces], c, 1)
    unit_down = by_owner([p[1] for p in pieces], c, 1)
    return jnp.stack([unit_up.reshape(unit_down.shape), unit_down])


def store_block(ids, i, block, refs):
    refs[0][...] = block


def column_pieces(ctx):

    def write(ids, i, block, refs):
        part = block.shape[1] // ctx
        for k in range(ctx):
            value = block[:, k * part : (k + 1) * part].astype(BF)
            put_piece_at(*refs, jnp.bitwise_xor(ids[0], k), value)

    return write


def kind_pieces(ctx):

    def write(ids, i, block, refs):
        part = block.shape[1] // 3
        for j in range(3):
            kind = lax.rem((j + 3 * ctx - ids[0]) * ctx, 3)
            value = block[:, :part]
            for k in range(1, 3):
                value = jnp.where(kind == k, block[:, k * part : (k + 1) * part], value)
            refs[j][...] = value.astype(BF)

    return write


def units_home(ids, up_pieces, down_pieces, up_shape, down_shape, sub, earlier=()):
    ctx = len(up_pieces)

    def kernel(ids, *refs):
        up_ref, down_ref = refs[2 * ctx :]
        ups = [ref[i] for ref, (_, i) in zip(refs, up_pieces)]
        downs = [ref[i] for ref, (_, i) in zip(refs[ctx:], down_pieces)]
        for k in range(ctx):
            down_ref[k * sub : (k + 1) * sub, :] = owned(ids, downs, k).astype(F32)
            value = owned(ids, ups, k).astype(F32)
            for i in range(value.shape[1] // sub):
                at = (i * ctx + k) * sub
                up_ref[:, at : at + sub] = value[:, i * sub : (i + 1) * sub]

    return call(
        kernel,
        [(up_shape, F32), (down_shape, F32)],
        [ids] + [array for array, _ in up_pieces + down_pieces],
        earlier=earlier,
    )


def add_result(middle, keep, got, bias, earlier=()):

    def kernel(ids, middle_ref, keep_ref, got_ref, bias_ref, out_ref):
        out_ref[...] = middle_ref[...] + keep_ref[...] + got_ref[...].astype(F32) + bias_ref[...]

    return call(
        kernel,
        [(middle.shape, F32)],
        [jnp.zeros((1,), jnp.int32), middle, keep, got, bias[None]],
        earlier=earlier,
    )[0]


def ctx_sum(x):
    for bit in reversed(ctx_bits(lax.axis_size("ctx"))):
        x = x + ctx_swap(x, bit)
    return x


def score_tile(q, k, slope, gap):
    return dot_nt(q, k) * (1.0 / math.sqrt(HEAD_DIM)) - slope * gap


def pair_gaps(pos_q, pos_k, seg_q, seg_k):
    allowed = (pos_k <= pos_q) & (seg_k == seg_q)
    return jnp.where(allowed, pos_q - pos_k, jnp.inf)


def attention_forward(ids, slopes, ln1_parts, full_qkv, qv_rows, tokens_col, tokens_row, unit):
    rows, width = ln1_parts[0].shape
    seq = rows * len(ln1_parts)
    tile = min(seq, 512)
    heads = unit // HEAD_DIM
    ctx = qv_rows.shape[0] // 2

    order = ctx_order(ctx)

    def kernel(ids, slopes, w_ref, bias_ref, col_ref, row_ref, *refs):
        x_ref, qkv_ref, attn_ref, lse_ref, near_ref, far_ref = refs[ctx:]
        for i in range(ctx):
            x_ref[i * rows : (i + 1) * rows, :] = refs[i][...]
        q_bias = bias_ref[pl.ds(ids[0], 1), :]
        v_bias = bias_ref[pl.ds(ctx + ids[0], 1), :]
        x = x_ref[...]
        qkv_ref[:, :unit] = (dot(x, w_ref[:, :unit]) + q_bias).astype(BF)
        qkv_ref[:, unit : 2 * unit] = dot(x, w_ref[:, unit : 2 * unit]).astype(BF)
        qkv_ref[:, 2 * unit :] = (dot(x, w_ref[:, 2 * unit :]) + v_bias).astype(BF)
        for lo in range(0, seq, tile):
            at = slice(lo, lo + tile)
            gap = pair_gaps(
                col_ref[at, 0:1], row_ref[0:1, :], col_ref[at, 1:2], row_ref[1:2, :]
            )
            for h in range(heads):
                cols = [slice(j * unit + h * HEAD_DIM, j * unit + (h + 1) * HEAD_DIM) for j in range(3)]
                scores = score_tile(qkv_ref[at, cols[0]], qkv_ref[:, cols[1]], slopes[h], gap)
                row_max = jnp.max(scores, axis=-1, keepdims=True)
                probs = jnp.exp(scores - row_max)
                row_sum = jnp.sum(probs, axis=-1, keepdims=True)
                out = dot(probs.astype(BF), qkv_ref[:, cols[2]]) / row_sum
                attn_ref[at, cols[0]] = out.astype(BF)
                lse_ref[at, h : h + 1] = row_max + jnp.log(row_sum)
        for i, r in enumerate(order):
            put_piece(near_ref, far_ref, r, attn_ref[i * rows : (i + 1) * rows, :])

    return call(
        kernel,
        [((seq, width), BF), ((seq, 3 * unit), BF), ((seq, unit), BF), ((seq, heads), F32)]
        + piece_shapes(ctx, rows, unit),
        [ids, slopes, full_qkv, qv_rows, tokens_col, tokens_row, *ln1_parts],
        scalars=2,
        work=20 * tile * seq,
    )


def attention_backward(
    ids, slopes, ln1_all, qkv, attn, pieces, lse, tokens_col, tokens_row, unit, dps, earlier=()
):
    seq, width = ln1_all.shape
    ctx = len(pieces)
    order = ctx_order(ctx)
    rows = seq // ctx
    tile = min(seq, 512)
    heads = unit // HEAD_DIM
    inv_root = 1.0 / math.sqrt(HEAD_DIM)

    def kernel(ids, slopes, x_ref, qkv_ref, attn_ref, lse_ref, col_ref, row_ref, *refs):
        out_ref, sum_ref, *block_refs, total_ref, grad_ref = refs[ctx:]
        for i, r in enumerate(order):
            grad_ref[i * rows : (i + 1) * rows, :] = refs[r][pieces[r][1]]
        for lo in range(0, seq, tile):
            at = slice(lo, lo + tile)
            gap = pair_gaps(
                col_ref[at, 0:1], row_ref[0:1, :], col_ref[at, 1:2], row_ref[1:2, :]
            )
            for h in range(heads):
                cols = [slice(j * unit + h * HEAD_DIM, j * unit + (h + 1) * HEAD_DIM) for j in range(3)]
                q, k, v = qkv_ref[at, cols[0]], qkv_ref[:, cols[1]], qkv_ref[:, cols[2]]
                do = grad_ref[at, cols[0]]
                delta = jnp.sum(
                    do.astype(F32) * attn_ref[at, cols[0]].astype(F32), axis=-1, keepdims=True
                )
                probs = jnp.exp(score_tile(q, k, slopes[h], gap) - lse_ref[at, h : h + 1])
                score_bf = (probs * (dot_nt(do, v) - delta)).astype(BF)
                total_ref[at, cols[0]] = inv_root * dot(score_bf, k)
                dk = inv_root * dot_tn(score_bf, q)
                dv = dot_tn(probs.astype(BF), do)
                if lo:
                    dk = dk + total_ref[:, cols[1]]
                    dv = dv + total_ref[:, cols[2]]
                total_ref[:, cols[1]] = dk
                total_ref[:, cols[2]] = dv
        total = total_ref[...]
        out_ref[...] = total.astype(BF)
        sum_ref[...] = jnp.sum(total, axis=0, keepdims=True)
        grad_blocks(ids, x_ref, out_ref[...], *block_refs)

    return call(
        kernel,
        [((seq, 3 * unit), BF), ((1, 3 * unit), F32)] + block_shapes(dps, width // dps, 3 * unit, 1),
        [ids, slopes, ln1_all, qkv, attn, lse, tokens_col, tokens_row]
        + [array for array, _ in pieces],
        scalars=2,
        work=28 * tile * seq,
        scratch=[pltpu.VMEM((seq, 3 * unit), F32), pltpu.VMEM((seq, unit), BF)],
        earlier=earlier,
    )


def split_halves(value, keep_ref, send_ref):
    half = keep_ref.shape[0]
    keep_ref[...] = value[:half]
    send_ref[...] = value[half:].astype(BF)


def input_terms(ids, x, weight, normed_parts, qkv_sums, sums2, up_sums, sub):
    rows, width = x.shape[0], weight.shape[0]
    ctx = len(normed_parts)
    unit = width // ctx
    part = rows // ctx
    units = up_sums.shape[1]
    small_rows = 8 + units * ctx // width

    def kernel(ids, x_ref, w_ref, qkv_ref, sums_ref, up_ref, *refs):
        normed_refs = refs[:ctx]
        keep_ref, send_ref, small_ref = refs[ctx:]
        terms = dot_nt(x_ref[...], w_ref[...])
        split_halves(terms, keep_ref, send_ref)
        gain = jnp.zeros((1, width), F32)
        for i in range(ctx):
            product = terms[i * part : (i + 1) * part] * normed_refs[i][...].astype(F32)
            gain = gain + jnp.sum(product, axis=0, keepdims=True)
        small_ref[0:1, :] = gain
        small_ref[1:2, :] = jnp.sum(terms, axis=0, keepdims=True)
        small_ref[4:5, :] = sums_ref[2:3, :]
        small_ref[5:6, :] = sums_ref[0:1, :]
        small_ref[6:7, :] = sums_ref[1:2, :]
        small_ref[7:8, :] = sums_ref[3:4, :]
        for k in range(ctx):
            mine = ids[0] == k
            at = slice(k * unit, (k + 1) * unit)
            small_ref[2:3, at] = jnp.where(mine, qkv_ref[:, :unit], 0.0)
            small_ref[3:4, at] = jnp.where(mine, qkv_ref[:, 2 * unit :], 0.0)
            for j in range(units // sub):
                row, col = divmod((j * ctx + k) * sub, width)
                value = jnp.where(mine, up_ref[:, j * sub : (j + 1) * sub], 0.0)
                small_ref[8 + row : 9 + row, col : col + sub] = value

    return call(
        kernel,
        [((rows // 2, width), F32), ((rows // 2, width), BF), ((small_rows, width), F32)],
        [ids, x, weight, qkv_sums, sums2, up_sums, *normed_parts],
        work=8 * rows * width,
    )


def feed_forward_hidden(ids, ln2_all, full_up, unit_bias, cot_all, dps):
    seq, width = ln2_all.shape
    units = full_up.shape[1]

    def kernel(ids, x_ref, up_ref, bias_ref, cot_ref, hidden_ref, slope_ref, *block_refs):
        forward, slope = gelu_both(dot(x_ref[...], up_ref[...]) + bias_ref[...])
        slope_ref[...] = slope
        hidden_ref[...] = forward.astype(BF)
        grad_blocks(ids, hidden_ref, cot_ref[...], *block_refs)

    return call(
        kernel,
        [((seq, units), BF), ((seq, units), F32)] + block_shapes(dps, units // dps, width, 2),
        [ids, ln2_all, full_up, unit_bias, cot_all],
        work=16 * seq * units,
    )


def feed_forward_grad(ids, slope, full_up, cot_all, full_down):
    seq, units = slope.shape
    width = cot_all.shape[1]

    def kernel(ids, slope_ref, up_ref, cot_ref, down_ref, pre_ref, sum_ref, keep_ref, send_ref):
        pre_grad = dot_nt(cot_ref[...], down_ref[...]) * slope_ref[...]
        sum_ref[...] = jnp.sum(pre_grad, axis=0, keepdims=True)
        pre_ref[...] = pre_grad.astype(BF)
        split_halves(dot_nt(pre_ref[...], up_ref[...]), keep_ref, send_ref)

    return call(
        kernel,
        [
            ((seq, units), BF),
            ((1, units), F32),
            ((seq // 2, width), F32),
            ((seq // 2, width), BF),
        ],
        [ids, slope, full_up, cot_all, full_down],
        work=12 * seq * units,
    )


def weight_blocks(ids, left, right, dps, parts, earlier=()):

    def kernel(ids, left_ref, right_ref, *block_refs):
        grad_blocks(ids, left_ref, right_ref[...], *block_refs)

    shapes = block_shapes(dps, left.shape[1] // dps, right.shape[1], parts)
    return call(kernel, shapes, [ids, left, right], earlier=earlier)


def out_blocks(ids, attn_parts, cols, dps, earlier=()):
    ctx = len(cols)
    order = ctx_order(ctx)
    rows, width = attn_parts[0].shape
    unit = cols[0][0].shape[2]

    def kernel(ids, *refs):
        *block_refs, left_ref, right_ref = refs[2 * ctx :]
        for i, r in enumerate(order):
            at = slice(i * rows, (i + 1) * rows)
            left_ref[at, :] = refs[i][...]
            right_ref[at, :] = refs[ctx + r][cols[r][1]]
        grad_blocks(ids, left_ref, right_ref[...], *block_refs)

    return call(
        kernel,
        block_shapes(dps, width // dps, unit, 1),
        [ids, *attn_parts] + [array for array, _ in cols],
        scratch=[pltpu.VMEM((ctx * rows, width), BF), pltpu.VMEM((ctx * rows, unit), BF)],
        earlier=earlier,
    )


def times_weight(x, weight, earlier=()):
    rows, width = x.shape[0], weight.shape[1]

    def kernel(ids, x_ref, w_ref, keep_ref, send_ref):
        split_halves(dot(x_ref[...], w_ref[...]), keep_ref, send_ref)

    return call(
        kernel,
        [((rows // 2, width), F32), ((rows // 2, width), BF)],
        [jnp.zeros((1,), jnp.int32), x, weight],
        earlier=earlier,
    )


def scatter_step(keep, got, earlier=()):
    rows, width = keep.shape

    def kernel(ids, keep_ref, got_ref, next_ref, send_ref):
        split_halves(keep_ref[...] + got_ref[...].astype(F32), next_ref, send_ref)

    return call(
        kernel,
        [((rows // 2, width), F32), ((rows // 2, width), BF)],
        [jnp.zeros((1,), jnp.int32), keep, got],
        earlier=earlier,
    )


def scatter_first(keep, send, earlier=()):
    for bit in list(reversed(ctx_bits(lax.axis_size("ctx"))))[:-1]:
        keep, send = scatter_step(keep, ctx_swap(send, bit), earlier)
    return keep, send


def scatter_rest(keep, send):
    return keep, ctx_swap(send, lax.axis_size("ctx") // 2)


def project_out(ids, pieces, out_parts, stream, out_bias, gain, offset):
    _, rows, unit = pieces[0][0].shape
    ctx = len(pieces)
    width = stream.shape[1]

    def kernel(ids, *refs):
        piece_refs, w_refs = refs[:ctx], refs[ctx : 2 * ctx]
        stream_ref, bias_ref, gain_ref, offset_ref = refs[2 * ctx : 2 * ctx + 4]
        attn_ref, middle_ref, normed_ref, inv_ref, act_ref = refs[2 * ctx + 4 :]
        got = [ref[i] for ref, (_, i) in zip(piece_refs, pieces)]
        for k in range(ctx):
            attn_ref[:, k * unit : (k + 1) * unit] = owned(ids, got, k)
        parts = [dot(attn_ref[...], w_refs[r][...]) for r in range(ctx)]
        for k in range(ctx):
            at = slice(k * unit, (k + 1) * unit)
            middle_ref[:, at] = stream_ref[:, at] + owned(ids, parts, k) + bias_ref[:, at]
        out, normed, inv_std = layer_norm(middle_ref[...], gain_ref[...], offset_ref[...])
        normed_ref[...] = normed
        inv_ref[...] = inv_std
        act_ref[...] = out.astype(BF)

    full = (rows, width)
    return call(
        kernel,
        [(full, BF), (full, F32), (full, F32), ((rows, 1), F32), (full, BF)],
        [ids]
        + [array for array, _ in pieces]
        + [*out_parts, stream, out_bias[None], gain[None], offset[None]],
    )


def middle_backward(ids, keep, got, normed, inv_std, gain, upstream, out_parts, earlier=()):
    rows, width = upstream.shape
    ctx = len(out_parts)
    unit = width // ctx

    def kernel(ids, keep_ref, got_ref, normed_ref, inv_ref, gain_ref, up_ref, *refs):
        w_refs = refs[:ctx]
        middle_ref, sum_ref, attn_near, attn_far, cols_near, cols_far = refs[ctx:]
        cols = []
        out_grad = keep_ref[...] + got_ref[...].astype(F32)
        normed = normed_ref[...]
        middle_grad = up_ref[...] + norm_backward(out_grad, normed, inv_ref[...], gain_ref[...])
        middle_ref[...] = middle_grad
        sum_ref[0:1, :] = jnp.sum(out_grad * normed, axis=0, keepdims=True)
        sum_ref[1:2, :] = jnp.sum(out_grad, axis=0, keepdims=True)
        sum_ref[2:3, :] = jnp.sum(middle_grad, axis=0, keepdims=True)
        sum_ref[3:4, :] = jnp.sum(up_ref[...], axis=0, keepdims=True)
        middle_bf = middle_grad.astype(BF)
        for r in range(ctx):
            owner = jnp.bitwise_xor(ids[0], r)
            value = middle_bf[:, :unit]
            for k in range(1, ctx):
                value = jnp.where(owner == k, middle_bf[:, k * unit : (k + 1) * unit], value)
            cols.append(value)
            put_piece(cols_near, cols_far, r, value)
        for r in range(ctx):
            at = pl.multiple_of(jnp.bitwise_xor(ids[0], r) * unit, unit)
            total = dot_nt(cols[0], w_refs[0][pl.ds(at, unit), :])
            for j in range(1, ctx):
                total = total + dot_nt(cols[j], w_refs[j][pl.ds(at, unit), :])
            put_piece(attn_near, attn_far, r, total.astype(BF))

    return call(
        kernel,
        [((rows, width), F32), ((4, width), F32)] + piece_shapes(ctx, rows, unit) * 2,
        [ids, keep, got, normed, inv_std, gain[None], upstream, *out_parts],
        far=[3, 6] + list(range(7, 7 + ctx)),
        earlier=earlier,
    )


def input_backward(keep, got, normed, inv_std, gain, middle_grad, earlier=()):
    rows, width = middle_grad.shape

    def kernel(ids, keep_ref, got_ref, normed_ref, inv_ref, gain_ref, mid_ref, out_ref):
        out_grad = keep_ref[...] + got_ref[...].astype(F32)
        out_ref[...] = mid_ref[...] + norm_backward(
            out_grad, normed_ref[...], inv_ref[...], gain_ref[...]
        )

    return call(
        kernel,
        [((rows, width), F32)],
        [jnp.zeros((1,), jnp.int32), keep, got, normed, inv_std, gain[None], middle_grad],
        earlier=earlier,
    )[0]


def per_device(
    layer_input,
    segment_ids,
    ln1_gain,
    ln1_bias,
    w_qkv,
    qv_bias,
    w_out,
    out_bias,
    ln2_gain,
    ln2_bias,
    w_up,
    up_bias,
    w_down,
    down_bias,
    cotangent,
):
    stream = layer_input[0]
    upstream = cotangent[0]
    seg_row = segment_ids[0]
    rows, width = stream.shape
    ctx = lax.axis_size("ctx")
    dps = lax.axis_size("dp")
    c = lax.axis_index("ctx")
    seq = rows * ctx
    unit = width // ctx
    heads = HEADS // ctx
    inv_root = 1.0 / math.sqrt(HEAD_DIM)
    ff = up_bias.shape[0]
    sub = ff // dps // ctx
    order = ctx_order(ctx)
    slots = [order.index(r) for r in range(ctx)]
    places = dp_places()

    took = [
        lax.ppermute(
            w_qkv[:, j * unit : (j + 1) * unit], "ctx", [(i, (3 * i + j) % ctx) for i in range(ctx)]
        )
        for j in range(3)
    ]
    took = jnp.stack(took)
    head_qkv = jnp.concatenate(
        [pick(took, (kind * ctx + c) % 3) for kind in range(3)] + [w_out], axis=1
    )
    normed1_out, normed1, inv_std1 = layer_norm(stream, ln1_gain, ln1_bias)
    ln1_act = normed1_out.astype(BF)
    cot_bf = upstream.astype(BF)
    w_up, w_down, ln1_act, cot_bf, normed1 = lax.optimization_barrier(
        (w_up, w_down, ln1_act, cot_bf, normed1, head_qkv)
    )[:5]

    z_count, y_count = dp_shape(dps)
    top, *lower = ctx_bits(ctx)
    first_cuts = [lambda b: b[:, : 3 * unit], lambda b: b[:, 3 * unit :]]
    first_full, out_sends, out_full, second_full = None, [], None, None
    moving = head_qkv
    unit_parts = unit_pieces(w_up, w_down, c, sub, unit)
    ln1_parts = [ln1_act]
    normed_parts = [normed1.astype(BF)]
    cot_parts = [cot_bf]
    both = travel = second = None
    for s in range(z_count):
        last = s == z_count - 1
        row = along_y(moving)
        if not last:
            moving = ring_z(moving)
        if out_sends:
            out_sends.append(ctx_swap(out_sends.pop(), top))
        if s == 0:
            ln1_parts = gather_step(ln1_parts, top)
            unit_parts = exchange_step(unit_parts, top)
        if s == 1 % z_count:
            for bit in lower:
                unit_parts = exchange_step(unit_parts, bit)
            for bit in lower:
                ln1_parts = gather_step(ln1_parts, bit)
            both = join_units(unit_parts, c, w_up.shape[0])
            normed_parts = gather_step(normed_parts, top)
        if s == 2 % z_count:
            for bit in lower:
                normed_parts = gather_step(normed_parts, bit)
        if last:
            cot_parts = gather_step(cot_parts, top)
            second = along_y(both)
            travel = ring_z(both)
        moving, row, out_sends, first_full, ln1_parts, normed_parts, cot_parts, unit_parts = (
            lax.optimization_barrier(
                (moving, row, out_sends, first_full, ln1_parts, normed_parts, cot_parts, unit_parts)
            )
        )
        if both is not None:
            both, travel, second, row = lax.optimization_barrier((both, travel, second, row))
        here = places[s * y_count : (s + 1) * y_count]
        first_full = assemble(first_full, row, here, first_cuts)
        out_sends.append(jnp.stack([b[:, 3 * unit :] for b in row]))
    full_qkv, col_out = first_full

    second_cuts = [lambda b: b[0], lambda b: b[1]]
    second_row = along_y(travel)
    travel = ring_z(travel)
    out_sends.append(ctx_swap(out_sends.pop(), top))

    ids = jnp.stack([c, lax.axis_index("dp")]).astype(jnp.int32)
    seg_blocks = seg_row.reshape(ctx, rows)
    seg = jnp.concatenate([pick(seg_blocks, c ^ r) for r in order]).astype(F32)
    pos = jnp.concatenate([(c ^ r) * rows + jnp.arange(rows, dtype=jnp.int32) for r in order])
    tokens_row = jnp.stack([pos.astype(F32), seg])
    tokens_col = tokens_row.T
    slopes = jnp.exp2(-8.0 * (c * heads + 1 + jnp.arange(heads)).astype(F32) / HEADS)

    ln1_all, qkv_heads, attn_heads, lse, attn_near, attn_far = attention_forward(
        ids, slopes, ln1_parts, full_qkv, qv_bias.reshape(2 * ctx, unit), tokens_col, tokens_row, unit
    )

    def heads_joined(got):
        return jnp.concatenate([got[r] for r in order], axis=0)

    second_full = assemble(None, second, places[:y_count], second_cuts)
    attn_near, attn_far, travel, second_row, out_sends, second_full = lax.optimization_barrier(
        (attn_near, attn_far, travel, second_row, out_sends, second_full)
    )
    pieces = trade(attn_near, attn_far)
    second_full = assemble(second_full, second_row, places[y_count : 2 * y_count], second_cuts)
    second_row = along_y(travel)
    travel = ring_z(travel)
    (out_got,) = assemble(
        None, [g[t] for g in out_sends for t in range(y_count)], places, [lambda b: b[...]]
    )
    out_parts = [col_out, out_got]
    for bit in lower:
        out_parts = gather_step(out_parts, bit)
        cot_parts = gather_step(cot_parts, bit)
    out_parts = [out_parts[slots[r]] for r in range(ctx)]
    attn, middle, normed2, inv_std2, ln2_act = project_out(
        ids, pieces, out_parts, stream, out_bias, ln2_gain, ln2_bias
    )
    ln2_parts = gather_step([ln2_act], top)
    ln2_parts, cot_parts, travel, second_row, second_full = lax.optimization_barrier(
        (ln2_parts, cot_parts, travel, second_row, second_full)
    )
    second_full = assemble(second_full, second_row, places[2 * y_count : 3 * y_count], second_cuts)
    if (z_count, y_count) == (4, 2):
        got = [travel, jnp.stack([ring_y(travel[0]), ring_z(second_row[1][1])])]
    else:
        got = along_y(travel)
    for bit in lower:
        ln2_parts = gather_step(ln2_parts, bit)
    ln2_all = jnp.concatenate(ln2_parts, axis=0)
    cot_all = jnp.concatenate(cot_parts, axis=0)
    full_up, full_down = assemble(second_full, got, places[3 * y_count :], second_cuts)
    full_up = full_up.reshape(width, dps * sub)
    unit_bias = pick(jnp.moveaxis(up_bias.reshape(dps, ctx, sub), 1, 0), c).reshape(1, dps * sub)
    hidden, slope, *grad_down = feed_forward_hidden(ids, ln2_all, full_up, unit_bias, cot_all, dps)
    pre_bf, up_bias_part, ln2_keep, ln2_send = feed_forward_grad(
        ids, slope, full_up, cot_all, full_down
    )
    ln2_keep, ln2_send = scatter_first(ln2_keep, ln2_send)
    ln2_keep, ln2_got = scatter_rest(ln2_keep, ln2_send)
    grad_up = weight_blocks(ids, ln2_all, pre_bf, dps, 2, earlier=[ln2_send])

    down, up = Reduction(grad_down), Reduction(grad_up)
    down_sent = down.step()
    middle_grad, sums2, grad_near, grad_far, col_near, col_far = middle_backward(
        ids,
        ln2_keep,
        ln2_got,
        normed2,
        inv_std2,
        ln2_gain,
        upstream,
        out_parts,
        earlier=[grad_up[0], down_sent],
    )
    grad_pieces = trade(grad_near, grad_far)
    qkv_bf, qkv_sums, *grad_qkv = attention_backward(
        ids,
        slopes,
        ln1_all,
        qkv_heads,
        attn_heads,
        grad_pieces,
        lse,
        tokens_col,
        tokens_row,
        unit,
        dps,
        earlier=[down.terms[1][0]],
    )
    qkv = Reduction(grad_qkv)
    ln1_keep, ln1_send, small = input_terms(
        ids, qkv_bf, full_qkv, normed_parts, qkv_sums, sums2, up_bias_part, sub
    )
    while down.bits:
        down.step(ln1_send)
    up.step(ln1_send)
    for bit in reversed(lower):
        small = small + ctx_swap(small, bit)
    ln1_keep, ln1_send = scatter_first(ln1_keep, ln1_send)

    ln1_keep, ln1_send, small = sync([], ln1_keep, ln1_send, small)
    ln1_keep, ln1_got = scatter_rest(ln1_keep, ln1_send)
    small_got = ctx_swap(small, top)
    cols = trade(col_near, col_far)

    cols_got, ln1_got, small_got = sync([down, up], [a for a, _ in cols], ln1_got, small_got)
    cols = [(a, i) for a, (_, i) in zip(cols_got, cols)]
    small = small + small_got
    bits = dp_bits()
    small_got = dp_swap(small, bits[0])
    attn_parts = gather_step([attn], top)
    while up.bits:
        up.step()
    input_grad = input_backward(ln1_keep, ln1_got, normed1, inv_std1, ln1_gain, middle_grad)
    result_keep, result_send = scatter_first(*times_weight(hidden, full_down, earlier=[ln1_got]))
    down_out = down.result(piece_shapes(ctx, sub, unit), column_pieces(ctx))

    attn_parts, small_got, result_keep, result_send, down_out = sync(
        [up, qkv], attn_parts, small_got, result_keep, result_send, down_out
    )
    qkv.step()
    small = small + small_got
    small_got = dp_swap(small, bits[1])
    for bit in lower:
        attn_parts = gather_step(attn_parts, bit)
    grad_out = out_blocks(ids, attn_parts, cols, dps)
    out = Reduction(grad_out)
    result_keep, result_got = scatter_rest(result_keep, result_send)
    up_rows = w_up.shape[0]
    up_out = up.result(piece_shapes(ctx, up_rows, dps * sub // ctx), column_pieces(ctx))
    up_home, down_home = trade(*up_out), trade(*down_out)

    up_got, down_got, result_got = sync(
        [qkv], [a for a, _ in up_home], [a for a, _ in down_home], result_got
    )
    up_home = [(a, i) for a, (_, i) in zip(up_got, up_home)]
    down_home = [(a, i) for a, (_, i) in zip(down_got, down_home)]
    while qkv.bits:
        qkv.step()
    out.step()
    shard_up, shard_down = units_home(
        ids, up_home, down_home, w_up.shape, w_down.shape, sub
    )
    result = add_result(middle, result_keep, result_got, down_bias)

    small_got, shard_up, shard_down, result = sync([qkv, out], small_got, shard_up, shard_down, result)
    qkv_out = qkv.result([((up_rows, unit), BF)] * 3, kind_pieces(ctx))
    while out.bits:
        out.step()
    small = small + small_got
    for bit in bits[2:]:
        small = small + dp_swap(small, bit)
    sum_out = out.result([((up_rows, unit), F32)], store_block)[0]

    shard_qkv = jnp.concatenate(
        [
            lax.ppermute(qkv_out[j], "ctx", [((3 * i + j) % ctx, i) for i in range(ctx)])
            for j in range(3)
        ],
        axis=1,
    ).astype(F32)

    return (
        result[None],
        input_grad[None],
        small[0],
        small[1],
        shard_qkv,
        small[2:4].reshape(2 * width),
        sum_out,
        small[4],
        small[5],
        small[6],
        shard_up,
        small[8:].reshape(ff),
        shard_down,
        small[7],
    )


def solution(mesh):
    tokens = P("dp", "ctx", None)
    weight = P("dp", "ctx")
    placed = (
        tokens,
        P("dp", None),
        P(),
        P(),
        weight,
        P(),
        weight,
        P(),
        P(),
        P(),
        weight,
        P(),
        weight,
        P(),
        tokens,
    )
    return jax.shard_map(
        per_device,
        mesh=mesh,
        in_specs=placed,
        out_specs=(
            tokens,
            tokens,
            P(),
            P(),
            weight,
            P(),
            weight,
            P(),
            P(),
            P(),
            weight,
            P(),
            weight,
            P(),
        ),
        check_vma=False,
    )
```

```python
import math

import jax
import jax.numpy as jnp
from jax import lax
from jax.experimental import pallas as pl
from jax.experimental.pallas import tpu as pltpu
from jax.sharding import PartitionSpec as P

HEADS = 16
HEAD_DIM = 64

epsilon = 1e-05
gelu_scale = 0.7978845608028654
cubic_term = 0.044715
neg_large = -1e30
BF = jnp.bfloat16
F32 = jnp.float32


def layer_norm(values, gain, offset):
    center = jnp.mean(values, axis=-1, keepdims=True)
    centered = values - center
    variance = jnp.mean(centered * centered, axis=-1, keepdims=True)
    inv_std = lax.rsqrt(variance + epsilon)
    normed = centered * inv_std
    return (normed * gain + offset, normed, inv_std)


def norm_backward(upstream, normed, inv_std, gain):
    scaled = upstream * gain
    return inv_std * (
        scaled
        - jnp.mean(scaled, axis=-1, keepdims=True)
        - normed * jnp.mean(scaled * normed, axis=-1, keepdims=True)
    )


def gelu_both(values):
    square = values * values
    tangent = jnp.tanh(gelu_scale * (values + cubic_term * values * square))
    forward = 0.5 * values * (1.0 + tangent)
    slope = 0.5 * (1.0 + tangent) + 0.5 * values * (1.0 - tangent * tangent) * gelu_scale * (
        1.0 + 3.0 * cubic_term * square
    )
    return forward, slope


def dot(a, b):
    return jnp.dot(a, b, preferred_element_type=F32)


def dot_nt(a, b):
    return lax.dot_general(a, b, (((1,), (1,)), ((), ())), preferred_element_type=F32)


def dot_tn(a, b):
    return lax.dot_general(a, b, (((0,), (0,)), ((), ())), preferred_element_type=F32)


def pick(stack, index):
    return lax.dynamic_index_in_dim(stack, index, 0, keepdims=False)


def ctx_bits(count):
    bits = []
    bit = count // 2
    while bit:
        bits.append(bit)
        bit //= 2
    return bits


def ctx_order(count):
    order = [0]
    for bit in ctx_bits(count):
        order = order + [r | bit for r in order]
    return order


def ctx_swap(x, bit):
    count = lax.axis_size("ctx")
    return lax.ppermute(x, "ctx", [(i, i ^ bit) for i in range(count)])


def gather_step(pieces, bit):
    return pieces + [ctx_swap(p, bit) for p in pieces]


def ctx_gather(x):
    pieces = [x]
    for bit in ctx_bits(lax.axis_size("ctx")):
        pieces = gather_step(pieces, bit)
    return jnp.concatenate(pieces, axis=0)


def ctx_scatter(x):
    for bit in reversed(ctx_bits(lax.axis_size("ctx"))):
        half = x.shape[0] // 2
        x = x[:half] + ctx_swap(x[half:].astype(BF), bit).astype(F32)
    return x


def exchange_step(pieces, bit):
    pieces = list(pieces)
    slots = [r for r in range(len(pieces)) if r & bit]
    got = ctx_swap(jnp.stack([pieces[r] for r in slots]), bit)
    for i, r in enumerate(slots):
        pieces[r] = got[i]
    return pieces


def ctx_exchange(pieces):
    for bit in ctx_bits(lax.axis_size("ctx")):
        pieces = exchange_step(pieces, bit)
    return pieces


def trade(near, far):
    count = 2 * near.shape[0]
    if count == 4:
        got = ctx_swap(far, 2)
        return [(near, 0), (ctx_swap(near, 1), 1), (got, 0), (ctx_swap(got, 1), 1)]
    pieces = ctx_exchange([*near, *far])
    return [(piece[None], 0) for piece in pieces]


def put_piece(near_ref, far_ref, r, value):
    half = near_ref.shape[0]
    (near_ref if r < half else far_ref)[r % half] = value


def put_piece_at(near_ref, far_ref, slot, value):
    half = near_ref.shape[0]

    @pl.when(slot < half)
    def _():
        near_ref[slot] = value

    @pl.when(slot >= half)
    def _():
        far_ref[slot - half] = value


def piece_shapes(ctx, rows, width):
    return [((ctx // 2, rows, width), BF)] * 2


def owned(ids, pieces, k):
    value = pieces[0]
    for r in range(1, len(pieces)):
        value = jnp.where(ids[0] == (k ^ r), pieces[r], value)
    return value


def by_owner(pieces, me, axis):
    stack = jnp.stack(pieces)
    return jnp.concatenate([pick(stack, me ^ k) for k in range(len(pieces))], axis=axis)


def dp_shape(count):
    z_count = 4 if count % 4 == 0 else count
    return z_count, count // z_count


def ring_z(x):
    count = lax.axis_size("dp")
    _, y_count = dp_shape(count)
    return lax.ppermute(x, "dp", [(i, (i + y_count) % count) for i in range(count)])


def ring_y(x):
    count = lax.axis_size("dp")
    _, y_count = dp_shape(count)
    return lax.ppermute(
        x, "dp", [(i, i // y_count * y_count + (i + 1) % y_count) for i in range(count)]
    )


def along_y(x):
    row = [x]
    for _ in range(dp_shape(lax.axis_size("dp"))[1] - 1):
        row.append(ring_y(row[-1]))
    return row


def dp_places(reverse=False):
    count = lax.axis_size("dp")
    z_count, y_count = dp_shape(count)
    me = lax.axis_index("dp")
    z, y = me // y_count, me % y_count
    places = []
    for s in range(z_count):
        for t in range(y_count):
            places.append((z + z_count - s) % z_count * y_count + (y + y_count - t) % y_count)
    return places


def after(x, *earlier):
    return lax.optimization_barrier((x, *earlier))[0]


def call(kernel, outs, args, scalars=1, scratch=(), work=0, earlier=(), far=()):
    used = len(args)
    sizes = [(x.shape, x.dtype) for x in args] + list(outs) + [(x.shape, x.dtype) for x in scratch]
    held = sum(math.prod(shape) * jnp.dtype(dtype).itemsize for shape, dtype in sizes)
    limit = held * 5 // 4 + work + 4 * 2**20
    first_out = used + len(earlier)
    fetched = [pltpu.VMEM(args[i].shape, args[i].dtype) for i in far]
    if far:
        fetched.append(pltpu.SemaphoreType.DMA((len(far),)))

    def body(*refs):
        ins, rest = list(refs[:used]), refs[first_out:]
        if far:
            rest, buffers, sem = rest[: -len(far) - 1], rest[-len(far) - 1 : -1], rest[-1]
            copies = [
                pltpu.make_async_copy(ins[i], buffer, sem.at[j])
                for j, (i, buffer) in enumerate(zip(far, buffers))
            ]
            for copy in copies:
                copy.start()
            for copy in copies:
                copy.wait()
            for i, buffer in zip(far, buffers):
                ins[i] = buffer
        kernel(*ins, *rest)

    def space(i):
        if i in far:
            return pltpu.HBM
        return pltpu.SMEM if i < scalars else pl.ANY if i >= used else pltpu.VMEM

    return pl.pallas_call(
        body,
        out_shape=[jax.ShapeDtypeStruct(shape, dtype) for shape, dtype in outs],
        in_specs=[pl.BlockSpec(memory_space=space(i)) for i in range(first_out)],
        out_specs=[pl.BlockSpec(memory_space=pltpu.VMEM)] * len(outs),
        scratch_shapes=[*scratch, *fetched],
        compiler_params=pltpu.CompilerParams(vmem_limit_bytes=limit),
    )(*args, *earlier)


def assemble(full, blocks, places, cuts):
    count, held = len(blocks), len(cuts)
    shapes = [cut(jnp.zeros(blocks[0].shape, BF)).shape for cut in cuts]
    total = lax.axis_size("dp")

    def kernel(place_ref, *refs):
        outs = refs[-held:]
        for i in range(count):
            for out_ref, cut, (rows, _) in zip(outs, cuts, shapes):
                at = pl.multiple_of(place_ref[i] * rows, rows)
                out_ref[pl.ds(at, rows), :] = cut(refs[i])

    return pl.pallas_call(
        kernel,
        out_shape=[jax.ShapeDtypeStruct((total * rows, width), BF) for rows, width in shapes],
        in_specs=[pl.BlockSpec(memory_space=pltpu.SMEM)]
        + [pl.BlockSpec(memory_space=pltpu.VMEM)] * (count + (held if full else 0)),
        out_specs=[pl.BlockSpec(memory_space=pltpu.VMEM)] * held,
        input_output_aliases={1 + count + j: j for j in range(held)} if full else {},
        compiler_params=pltpu.CompilerParams(
            vmem_limit_bytes=4 * 2**20 + 6 * sum(total * rows * width for rows, width in shapes)
        ),
    )(jnp.stack(places).astype(jnp.int32), *blocks, *(full or []))


def dp_bits():
    bits = []
    bit = 1
    while bit < lax.axis_size("dp"):
        bits.append(bit)
        bit *= 2
    return bits


def slot_order(bits):
    order = [0]
    for bit in reversed(bits):
        order = order + [r | bit for r in order]
    return order


def grad_blocks(ids, left_ref, right, keep_ref, *send_refs):
    half, rows = keep_ref.shape[:2]
    bits = []
    while 2 ** len(bits) < 2 * half:
        bits.append(2 ** len(bits))
    ranges = [(keep_ref, 0)]
    for ref in send_refs[::-1]:
        ranges.append((ref, ranges[-1][1] + ranges[-1][0].shape[0]))
    for k in range(2 * half):
        block = dot_tn(left_ref[:, k * rows : (k + 1) * rows], right).astype(BF)
        name = jnp.bitwise_xor(ids[1], k)
        slot = 0
        for i, bit in enumerate(bits):
            slot = slot + lax.div(jnp.bitwise_and(name, bit), bit) * (half >> i)
        for ref, first in ranges:

            @pl.when((slot >= first) & (slot < first + ref.shape[0]))
            def _():
                ref[slot - first] = block


def block_shapes(dps, rows, width, parts):
    half = dps // 2
    counts = [half] + ([half] if parts == 1 else [half - half // 2, half // 2])
    return [((n, rows, width), BF) for n in counts]


def dp_swap(x, bit):
    count = lax.axis_size("dp")
    return lax.ppermute(x, "dp", [(i, i ^ bit) for i in range(count)])


def combine(terms, start, count, outs, write, earlier=()):

    def kernel(ids, *refs):
        for i in range(count):
            total = refs[0][start - terms[0][1] + i].astype(F32)
            for ref, (_, first) in zip(refs[1 : len(terms)], terms[1:]):
                total = total + ref[start - first + i].astype(F32)
            write(ids, i, total, refs[len(terms) :])

    ids = lax.axis_index("ctx").astype(jnp.int32)[None]
    return call(kernel, outs, [ids] + [array for array, _ in terms], earlier=earlier)


class Reduction:

    def __init__(self, blocks):
        keep, *sends = blocks
        self.bits = dp_bits()
        self.size = keep.shape[0]
        bit = self.bits.pop(0)
        got = [dp_swap(send, bit) for send in sends]
        self.first = [(keep, 0), (got[0], self.size - got[0].shape[0])]
        self.terms = [(keep, 0), (got[-1], 0)]

    def step(self, *earlier):
        self.size //= 2
        terms, self.first = self.first or self.terms, None
        last = len(self.bits) == 1

        def write(ids, i, block, refs):
            refs[0][i] = block.astype(BF)

        def write_both(ids, i, block, refs):
            if i:
                refs[0][0] = block.astype(BF)
            else:
                refs[1][0] = block

        block = terms[0][0].shape[1:]
        if last and terms is self.terms:
            outs = [((1,) + block, BF), ((1,) + block, F32)]
            send, own = combine(terms, 0, 2, outs, write_both, earlier)
            self.terms = [(own, 0)]
        else:
            outs = [((self.size,) + block, BF)]
            (send,) = combine(terms, self.size, self.size, outs, write, earlier)
        self.terms.append((dp_swap(send, self.bits.pop(0)), 0))
        return send

    def result(self, outs, write, *earlier):
        return combine(self.terms, 0, 1, outs, write, earlier)


def sync(reductions, *values):
    held = [([a for a, _ in r.first or []], [a for a, _ in r.terms]) for r in reductions]
    held, values = lax.optimization_barrier((held, values))
    for r, (first, terms) in zip(reductions, held):
        if r.first:
            r.first = [(a, at) for a, (_, at) in zip(first, r.first)]
        r.terms = [(a, at) for a, (_, at) in zip(terms, r.terms)]
    return values


def unit_pieces(w_up, w_down, c, sub, unit):
    ctx, dps = lax.axis_size("ctx"), lax.axis_size("dp")
    down_view = w_down.reshape(ctx, sub, unit)
    up_view = jnp.moveaxis(w_up.reshape(w_up.shape[0], dps // ctx, ctx, sub), 2, 0).reshape(
        ctx, sub, unit
    )
    return [jnp.stack([pick(up_view, c ^ r), pick(down_view, c ^ r)]) for r in range(ctx)]


def join_units(pieces, c, up_rows):
    unit_up = by_owner([p[0].reshape(up_rows, -1) for p in pieces], c, 1)
    unit_down = by_owner([p[1] for p in pieces], c, 1)
    return jnp.stack([unit_up.reshape(unit_down.shape), unit_down])


def store_block(ids, i, block, refs):
    refs[0][...] = block


def column_pieces(ctx):

    def write(ids, i, block, refs):
        part = block.shape[1] // ctx
        for k in range(ctx):
            value = block[:, k * part : (k + 1) * part].astype(BF)
            put_piece_at(*refs, jnp.bitwise_xor(ids[0], k), value)

    return write


def units_home(ids, up_pieces, down_pieces, up_shape, down_shape, sub, earlier=()):
    ctx = len(up_pieces)

    def kernel(ids, *refs):
        up_ref, down_ref = refs[2 * ctx :]
        ups = [ref[i] for ref, (_, i) in zip(refs, up_pieces)]
        downs = [ref[i] for ref, (_, i) in zip(refs[ctx:], down_pieces)]
        for k in range(ctx):
            down_ref[k * sub : (k + 1) * sub, :] = owned(ids, downs, k).astype(F32)
            value = owned(ids, ups, k).astype(F32)
            for i in range(value.shape[1] // sub):
                at = (i * ctx + k) * sub
                up_ref[:, at : at + sub] = value[:, i * sub : (i + 1) * sub]

    return call(
        kernel,
        [(up_shape, F32), (down_shape, F32)],
        [ids] + [array for array, _ in up_pieces + down_pieces],
        earlier=earlier,
    )


def add_result(middle, keep, got, bias, earlier=()):

    def kernel(ids, middle_ref, keep_ref, got_ref, bias_ref, out_ref):
        out_ref[...] = middle_ref[...] + keep_ref[...] + got_ref[...].astype(F32) + bias_ref[...]

    return call(
        kernel,
        [(middle.shape, F32)],
        [jnp.zeros((1,), jnp.int32), middle, keep, got, bias[None]],
        earlier=earlier,
    )[0]


def ctx_sum(x):
    for bit in reversed(ctx_bits(lax.axis_size("ctx"))):
        x = x + ctx_swap(x, bit)
    return x


def score_tile(q, k, slope, gap):
    return dot_nt(q, k) * (1.0 / math.sqrt(HEAD_DIM)) - slope * gap


def pair_gaps(pos_q, pos_k, seg_q, seg_k):
    allowed = (pos_k <= pos_q) & (seg_k == seg_q)
    return jnp.where(allowed, pos_q - pos_k, jnp.inf)


def attention_forward(ids, slopes, ln1_parts, full_qkv, qv_rows, tokens_col, tokens_row, unit):
    rows, width = ln1_parts[0].shape
    seq = rows * len(ln1_parts)
    tile = min(seq, 512)
    heads = unit // HEAD_DIM
    ctx = qv_rows.shape[0] // 2

    order = ctx_order(ctx)

    def kernel(ids, slopes, w_ref, bias_ref, col_ref, row_ref, *refs):
        x_ref, qkv_ref, attn_ref, lse_ref, near_ref, far_ref = refs[ctx:]
        for i in range(ctx):
            x_ref[i * rows : (i + 1) * rows, :] = refs[i][...]
        q_bias = bias_ref[pl.ds(ids[0], 1), :]
        v_bias = bias_ref[pl.ds(ctx + ids[0], 1), :]
        x = x_ref[...]
        qkv_ref[:, :unit] = (dot(x, w_ref[:, :unit]) + q_bias).astype(BF)
        qkv_ref[:, unit : 2 * unit] = dot(x, w_ref[:, unit : 2 * unit]).astype(BF)
        qkv_ref[:, 2 * unit :] = (dot(x, w_ref[:, 2 * unit :]) + v_bias).astype(BF)
        for lo in range(0, seq, tile):
            at = slice(lo, lo + tile)
            gap = pair_gaps(
                col_ref[at, 0:1], row_ref[0:1, :], col_ref[at, 1:2], row_ref[1:2, :]
            )
            for h in range(heads):
                cols = [slice(j * unit + h * HEAD_DIM, j * unit + (h + 1) * HEAD_DIM) for j in range(3)]
                scores = score_tile(qkv_ref[at, cols[0]], qkv_ref[:, cols[1]], slopes[h], gap)
                row_max = jnp.max(scores, axis=-1, keepdims=True)
                probs = jnp.exp(scores - row_max)
                row_sum = jnp.sum(probs, axis=-1, keepdims=True)
                out = dot(probs.astype(BF), qkv_ref[:, cols[2]]) / row_sum
                attn_ref[at, cols[0]] = out.astype(BF)
                lse_ref[at, h : h + 1] = row_max + jnp.log(row_sum)
        for i, r in enumerate(order):
            put_piece(near_ref, far_ref, r, attn_ref[i * rows : (i + 1) * rows, :])

    return call(
        kernel,
        [((seq, width), BF), ((seq, 3 * unit), BF), ((seq, unit), BF), ((seq, heads), F32)]
        + piece_shapes(ctx, rows, unit),
        [ids, slopes, full_qkv, qv_rows, tokens_col, tokens_row, *ln1_parts],
        scalars=2,
        work=20 * tile * seq,
    )


def attention_backward(
    ids, slopes, qkv, attn, pieces, lse, tokens_col, tokens_row, unit, earlier=()
):
    seq = qkv.shape[0]
    ctx = len(pieces)
    order = ctx_order(ctx)
    rows = seq // ctx
    tile = min(seq, 512)
    heads = unit // HEAD_DIM
    inv_root = 1.0 / math.sqrt(HEAD_DIM)

    def kernel(ids, slopes, qkv_ref, attn_ref, lse_ref, col_ref, row_ref, *refs):
        out_ref, sum_ref, *kind_refs, total_ref, grad_ref = refs[ctx:]
        for i, r in enumerate(order):
            grad_ref[i * rows : (i + 1) * rows, :] = refs[r][pieces[r][1]]
        for lo in range(0, seq, tile):
            at = slice(lo, lo + tile)
            gap = pair_gaps(
                col_ref[at, 0:1], row_ref[0:1, :], col_ref[at, 1:2], row_ref[1:2, :]
            )
            for h in range(heads):
                cols = [slice(j * unit + h * HEAD_DIM, j * unit + (h + 1) * HEAD_DIM) for j in range(3)]
                q, k, v = qkv_ref[at, cols[0]], qkv_ref[:, cols[1]], qkv_ref[:, cols[2]]
                do = grad_ref[at, cols[0]]
                delta = jnp.sum(
                    do.astype(F32) * attn_ref[at, cols[0]].astype(F32), axis=-1, keepdims=True
                )
                probs = jnp.exp(score_tile(q, k, slopes[h], gap) - lse_ref[at, h : h + 1])
                score_bf = (probs * (dot_nt(do, v) - delta)).astype(BF)
                total_ref[at, cols[0]] = inv_root * dot(score_bf, k)
                dk = inv_root * dot_tn(score_bf, q)
                dv = dot_tn(probs.astype(BF), do)
                if lo:
                    dk = dk + total_ref[:, cols[1]]
                    dv = dv + total_ref[:, cols[2]]
                total_ref[:, cols[1]] = dk
                total_ref[:, cols[2]] = dv
        total = total_ref[...]
        out_ref[...] = total.astype(BF)
        sum_ref[...] = jnp.sum(total, axis=0, keepdims=True)
        for j in range(3):
            slot = j
            if ctx == 4 and j != 1:
                slot = jnp.where(lax.rem(ids[0], 2) == 0, j, 2 - j)
            kind = lax.rem((slot + 3 * ctx - ids[0]) * ctx, 3)
            value = out_ref[:, :unit]
            for k in range(1, 3):
                value = jnp.where(kind == k, out_ref[:, k * unit : (k + 1) * unit], value)
            kind_refs[j][...] = value

    return call(
        kernel,
        [((seq, 3 * unit), BF), ((1, 3 * unit), F32)] + [((seq, unit), BF)] * 3,
        [ids, slopes, qkv, attn, lse, tokens_col, tokens_row]
        + [array for array, _ in pieces],
        scalars=2,
        work=28 * tile * seq,
        scratch=[pltpu.VMEM((seq, 3 * unit), F32), pltpu.VMEM((seq, unit), BF)],
        earlier=earlier,
    )


def split_halves(value, keep_ref, send_ref):
    half = keep_ref.shape[0]
    keep_ref[...] = value[:half]
    send_ref[...] = value[half:].astype(BF)


def input_terms(ids, x, weight, normed_parts, qkv_sums, sums2, up_sums, sub):
    rows, width = x.shape[0], weight.shape[0]
    ctx = len(normed_parts)
    unit = width // ctx
    part = rows // ctx
    units = up_sums.shape[1]
    small_rows = 8 + units * ctx // width

    def kernel(ids, x_ref, w_ref, qkv_ref, sums_ref, up_ref, *refs):
        normed_refs = refs[:ctx]
        keep_ref, send_ref, small_ref = refs[ctx:]
        terms = dot_nt(x_ref[...], w_ref[...])
        split_halves(terms, keep_ref, send_ref)
        gain = jnp.zeros((1, width), F32)
        for i in range(ctx):
            product = terms[i * part : (i + 1) * part] * normed_refs[i][...].astype(F32)
            gain = gain + jnp.sum(product, axis=0, keepdims=True)
        small_ref[0:1, :] = gain
        small_ref[1:2, :] = jnp.sum(terms, axis=0, keepdims=True)
        small_ref[4:5, :] = sums_ref[2:3, :]
        small_ref[5:6, :] = sums_ref[0:1, :]
        small_ref[6:7, :] = sums_ref[1:2, :]
        small_ref[7:8, :] = sums_ref[3:4, :]
        for k in range(ctx):
            mine = ids[0] == k
            at = slice(k * unit, (k + 1) * unit)
            small_ref[2:3, at] = jnp.where(mine, qkv_ref[:, :unit], 0.0)
            small_ref[3:4, at] = jnp.where(mine, qkv_ref[:, 2 * unit :], 0.0)
            for j in range(units // sub):
                row, col = divmod((j * ctx + k) * sub, width)
                value = jnp.where(mine, up_ref[:, j * sub : (j + 1) * sub], 0.0)
                small_ref[8 + row : 9 + row, col : col + sub] = value

    return call(
        kernel,
        [((rows // 2, width), F32), ((rows // 2, width), BF), ((small_rows, width), F32)],
        [ids, x, weight, qkv_sums, sums2, up_sums, *normed_parts],
        work=8 * rows * width,
    )


def feed_forward_hidden(ids, ln2_parts, full_up, unit_bias, cot_parts, dps, earlier=()):
    ctx = len(ln2_parts)
    rows, width = ln2_parts[0].shape
    seq = rows * ctx
    units = full_up.shape[1]

    def kernel(ids, up_ref, bias_ref, *refs):
        x_ref, cot_ref, hidden_ref, slope_ref, *block_refs = refs[2 * ctx :]
        for i in range(ctx):
            x_ref[i * rows : (i + 1) * rows, :] = refs[i][...]
            cot_ref[i * rows : (i + 1) * rows, :] = refs[ctx + i][...]
        forward, slope = gelu_both(dot(x_ref[...], up_ref[...]) + bias_ref[...])
        slope_ref[...] = slope
        hidden_ref[...] = forward.astype(BF)
        grad_blocks(ids, hidden_ref, cot_ref[...], *block_refs)

    return call(
        kernel,
        [((seq, width), BF), ((seq, width), BF), ((seq, units), BF), ((seq, units), F32)]
        + block_shapes(dps, units // dps, width, 2),
        [ids, full_up, unit_bias, *ln2_parts, *cot_parts],
        work=16 * seq * units,
        earlier=earlier,
    )


def feed_forward_grad(ids, slope, full_up, cot_all, full_down):
    seq, units = slope.shape
    width = cot_all.shape[1]

    def kernel(ids, slope_ref, up_ref, cot_ref, down_ref, pre_ref, sum_ref, keep_ref, send_ref):
        pre_grad = dot_nt(cot_ref[...], down_ref[...]) * slope_ref[...]
        sum_ref[...] = jnp.sum(pre_grad, axis=0, keepdims=True)
        pre_ref[...] = pre_grad.astype(BF)
        split_halves(dot_nt(pre_ref[...], up_ref[...]), keep_ref, send_ref)

    return call(
        kernel,
        [
            ((seq, units), BF),
            ((1, units), F32),
            ((seq // 2, width), F32),
            ((seq // 2, width), BF),
        ],
        [ids, slope, full_up, cot_all, full_down],
        work=12 * seq * units,
    )


def weight_blocks(ids, left, right, dps, parts, earlier=()):

    def kernel(ids, left_ref, right_ref, *block_refs):
        grad_blocks(ids, left_ref, right_ref[...], *block_refs)

    shapes = block_shapes(dps, left.shape[1] // dps, right.shape[1], parts)
    return call(kernel, shapes, [ids, left, right], earlier=earlier)


def out_blocks(ids, attn_parts, cols, dps, earlier=()):
    ctx = len(cols)
    order = ctx_order(ctx)
    rows, width = attn_parts[0].shape
    unit = cols[0][0].shape[2]

    def kernel(ids, *refs):
        *block_refs, left_ref, right_ref = refs[2 * ctx :]
        for i, r in enumerate(order):
            at = slice(i * rows, (i + 1) * rows)
            left_ref[at, :] = refs[i][...]
            right_ref[at, :] = refs[ctx + r][cols[r][1]]
        grad_blocks(ids, left_ref, right_ref[...], *block_refs)

    return call(
        kernel,
        block_shapes(dps, width // dps, unit, 1),
        [ids, *attn_parts] + [array for array, _ in cols],
        scratch=[pltpu.VMEM((ctx * rows, width), BF), pltpu.VMEM((ctx * rows, unit), BF)],
        earlier=earlier,
    )


def unit_blocks(ids, left, kinds, dps):
    seq, width = left.shape
    unit = kinds[0].shape[1]
    ctx = width // unit
    rows = seq // ctx
    bits = ctx_bits(ctx)

    def kernel(ids, left_ref, *refs):
        kind_refs, block_refs, right_ref = refs[:3], refs[3:-1], refs[-1]
        if ctx == 4:
            even = lax.rem(ids[0], 2) == 0
            for i in range(ctx):
                at = slice(i * rows, (i + 1) * rows)
                stayed = kind_refs[0][at, :]
                crossed = kind_refs[2][(i ^ 1) * rows : ((i ^ 1) + 1) * rows, :]
                right_ref[at, :unit] = jnp.where(even, stayed, crossed)
                right_ref[at, unit : 2 * unit] = kind_refs[1][
                    (i ^ 2) * rows : ((i ^ 2) + 1) * rows, :
                ]
                right_ref[at, 2 * unit :] = jnp.where(even, crossed, stayed)
        for j in range(3 if ctx != 4 else 0):
            apart = jnp.bitwise_xor(ids[0], lax.rem(3 * ids[0] + j, ctx))
            shift = 0
            for i, bit in enumerate(bits):
                shift = shift + lax.div(jnp.bitwise_and(apart, bit), bit) * (1 << i)
            for i in range(ctx):
                at = pl.multiple_of(jnp.bitwise_xor(shift, i) * rows, rows)
                right_ref[i * rows : (i + 1) * rows, j * unit : (j + 1) * unit] = kind_refs[j][
                    pl.ds(at, rows), :
                ]
        grad_blocks(ids, left_ref, right_ref[...], *block_refs)

    return call(
        kernel,
        block_shapes(dps, width // dps, 3 * unit, 1),
        [ids, left, *kinds],
        scratch=[pltpu.VMEM((seq, 3 * unit), BF)],
    )


def unit_columns_home(slots, c):
    ctx = lax.axis_size("ctx")
    if ctx != 4:
        return [
            lax.ppermute(slots[j], "ctx", [((3 * i + j) % ctx, i) for i in range(ctx)])
            for j in range(3)
        ]
    return [slots[0], ctx_swap(slots[1], 1), ctx_swap(slots[2], 2)]


def times_weight(x, weight, earlier=()):
    rows, width = x.shape[0], weight.shape[1]

    def kernel(ids, x_ref, w_ref, keep_ref, send_ref):
        split_halves(dot(x_ref[...], w_ref[...]), keep_ref, send_ref)

    return call(
        kernel,
        [((rows // 2, width), F32), ((rows // 2, width), BF)],
        [jnp.zeros((1,), jnp.int32), x, weight],
        earlier=earlier,
    )


def scatter_step(keep, got, earlier=()):
    rows, width = keep.shape

    def kernel(ids, keep_ref, got_ref, next_ref, send_ref):
        split_halves(keep_ref[...] + got_ref[...].astype(F32), next_ref, send_ref)

    return call(
        kernel,
        [((rows // 2, width), F32), ((rows // 2, width), BF)],
        [jnp.zeros((1,), jnp.int32), keep, got],
        earlier=earlier,
    )


def scatter_first(keep, send, earlier=()):
    for bit in list(reversed(ctx_bits(lax.axis_size("ctx"))))[:-1]:
        keep, send = scatter_step(keep, ctx_swap(send, bit), earlier)
    return keep, send


def scatter_rest(keep, send):
    return keep, ctx_swap(send, lax.axis_size("ctx") // 2)


def project_out(ids, pieces, out_parts, stream, out_bias, gain, offset):
    _, rows, unit = pieces[0][0].shape
    ctx = len(pieces)
    width = stream.shape[1]

    def kernel(ids, *refs):
        piece_refs, w_refs = refs[:ctx], refs[ctx : 2 * ctx]
        stream_ref, bias_ref, gain_ref, offset_ref = refs[2 * ctx : 2 * ctx + 4]
        attn_ref, middle_ref, normed_ref, inv_ref, act_ref = refs[2 * ctx + 4 :]
        got = [ref[i] for ref, (_, i) in zip(piece_refs, pieces)]
        for k in range(ctx):
            attn_ref[:, k * unit : (k + 1) * unit] = owned(ids, got, k)
        parts = [dot(attn_ref[...], w_refs[r][...]) for r in range(ctx)]
        for k in range(ctx):
            at = slice(k * unit, (k + 1) * unit)
            middle_ref[:, at] = stream_ref[:, at] + owned(ids, parts, k) + bias_ref[:, at]
        out, normed, inv_std = layer_norm(middle_ref[...], gain_ref[...], offset_ref[...])
        normed_ref[...] = normed
        inv_ref[...] = inv_std
        act_ref[...] = out.astype(BF)

    full = (rows, width)
    return call(
        kernel,
        [(full, BF), (full, F32), (full, F32), ((rows, 1), F32), (full, BF)],
        [ids]
        + [array for array, _ in pieces]
        + [*out_parts, stream, out_bias[None], gain[None], offset[None]],
    )


def middle_backward(ids, keep, got, normed, inv_std, gain, upstream, out_parts, earlier=()):
    rows, width = upstream.shape
    ctx = len(out_parts)
    unit = width // ctx

    def kernel(ids, keep_ref, got_ref, normed_ref, inv_ref, gain_ref, up_ref, *refs):
        w_refs = refs[:ctx]
        middle_ref, sum_ref, attn_near, attn_far, cols_near, cols_far = refs[ctx:]
        cols = []
        out_grad = keep_ref[...] + got_ref[...].astype(F32)
        normed = normed_ref[...]
        middle_grad = up_ref[...] + norm_backward(out_grad, normed, inv_ref[...], gain_ref[...])
        middle_ref[...] = middle_grad
        sum_ref[0:1, :] = jnp.sum(out_grad * normed, axis=0, keepdims=True)
        sum_ref[1:2, :] = jnp.sum(out_grad, axis=0, keepdims=True)
        sum_ref[2:3, :] = jnp.sum(middle_grad, axis=0, keepdims=True)
        sum_ref[3:4, :] = jnp.sum(up_ref[...], axis=0, keepdims=True)
        middle_bf = middle_grad.astype(BF)
        for r in range(ctx):
            owner = jnp.bitwise_xor(ids[0], r)
            value = middle_bf[:, :unit]
            for k in range(1, ctx):
                value = jnp.where(owner == k, middle_bf[:, k * unit : (k + 1) * unit], value)
            cols.append(value)
            put_piece(cols_near, cols_far, r, value)
        for r in range(ctx):
            at = pl.multiple_of(jnp.bitwise_xor(ids[0], r) * unit, unit)
            total = dot_nt(cols[0], w_refs[0][pl.ds(at, unit), :])
            for j in range(1, ctx):
                total = total + dot_nt(cols[j], w_refs[j][pl.ds(at, unit), :])
            put_piece(attn_near, attn_far, r, total.astype(BF))

    return call(
        kernel,
        [((rows, width), F32), ((4, width), F32)] + piece_shapes(ctx, rows, unit) * 2,
        [ids, keep, got, normed, inv_std, gain[None], upstream, *out_parts],
        far=[3, 6] + list(range(7, 7 + ctx)),
        earlier=earlier,
    )


def input_backward(keep, got, normed, inv_std, gain, middle_grad, earlier=()):
    rows, width = middle_grad.shape

    def kernel(ids, keep_ref, got_ref, normed_ref, inv_ref, gain_ref, mid_ref, out_ref):
        out_grad = keep_ref[...] + got_ref[...].astype(F32)
        out_ref[...] = mid_ref[...] + norm_backward(
            out_grad, normed_ref[...], inv_ref[...], gain_ref[...]
        )

    return call(
        kernel,
        [((rows, width), F32)],
        [jnp.zeros((1,), jnp.int32), keep, got, normed, inv_std, gain[None], middle_grad],
        earlier=earlier,
    )[0]


def per_device(
    layer_input,
    segment_ids,
    ln1_gain,
    ln1_bias,
    w_qkv,
    qv_bias,
    w_out,
    out_bias,
    ln2_gain,
    ln2_bias,
    w_up,
    up_bias,
    w_down,
    down_bias,
    cotangent,
):
    stream = layer_input[0]
    upstream = cotangent[0]
    seg_row = segment_ids[0]
    rows, width = stream.shape
    ctx = lax.axis_size("ctx")
    dps = lax.axis_size("dp")
    c = lax.axis_index("ctx")
    seq = rows * ctx
    unit = width // ctx
    heads = HEADS // ctx
    inv_root = 1.0 / math.sqrt(HEAD_DIM)
    ff = up_bias.shape[0]
    sub = ff // dps // ctx
    order = ctx_order(ctx)
    slots = [order.index(r) for r in range(ctx)]
    places = dp_places()

    if ctx == 4:
        odd = c % 2
        trio = w_qkv.reshape(w_qkv.shape[0], 3, unit)
        stays = lax.dynamic_index_in_dim(trio, 2 * odd, 1, keepdims=False)
        crossed = ctx_swap(lax.dynamic_index_in_dim(trio, 2 - 2 * odd, 1, keepdims=False), 2)
        beside = ctx_swap(trio[:, 1], 1)
        three = jnp.stack([stays, crossed, beside])
        held = [(0, 2, 1), (2, 0, 1), (1, 0, 2), (1, 2, 0)]
        place = [
            sum(jnp.where(c == k, held[k][kind], 0) for k in range(4)) for kind in range(3)
        ]
        head_qkv = jnp.concatenate([pick(three, at) for at in place] + [w_out], axis=1)
    else:
        took = [
            lax.ppermute(
                w_qkv[:, j * unit : (j + 1) * unit],
                "ctx",
                [(i, (3 * i + j) % ctx) for i in range(ctx)],
            )
            for j in range(3)
        ]
        took = jnp.stack(took)
        head_qkv = jnp.concatenate(
            [pick(took, (kind * ctx + c) % 3) for kind in range(3)] + [w_out], axis=1
        )

    normed1_out, normed1, inv_std1 = layer_norm(stream, ln1_gain, ln1_bias)
    ln1_act = normed1_out.astype(BF)
    cot_bf = upstream.astype(BF)
    w_up, w_down, ln1_act, cot_bf, normed1 = lax.optimization_barrier(
        (w_up, w_down, ln1_act, cot_bf, normed1, head_qkv)
    )[:5]

    z_count, y_count = dp_shape(dps)
    top, *lower = ctx_bits(ctx)
    first_cuts = [lambda b: b[:, : 3 * unit], lambda b: b[:, 3 * unit :]]
    first_full, out_sends, out_full, second_full = None, [], None, None
    moving = head_qkv
    unit_parts = unit_pieces(w_up, w_down, c, sub, unit)
    ln1_parts = [ln1_act]
    normed_parts = [normed1.astype(BF)]
    cot_parts = [cot_bf]
    both = travel = second = None
    for s in range(z_count):
        last = s == z_count - 1
        row = along_y(moving)
        if not last:
            moving = ring_z(moving)
        if out_sends:
            out_sends.append(ctx_swap(out_sends.pop(), top))
        if s == 0:
            ln1_parts = gather_step(ln1_parts, top)
            unit_parts = exchange_step(unit_parts, top)
        if s == 1 % z_count:
            for bit in lower:
                unit_parts = exchange_step(unit_parts, bit)
            for bit in lower:
                ln1_parts = gather_step(ln1_parts, bit)
            both = join_units(unit_parts, c, w_up.shape[0])
            normed_parts = gather_step(normed_parts, top)
        if s == 2 % z_count:
            for bit in lower:
                normed_parts = gather_step(normed_parts, bit)
        if last:
            cot_parts = gather_step(cot_parts, top)
            second = along_y(both)
            travel = ring_z(both)
        moving, row, out_sends, first_full, ln1_parts, normed_parts, cot_parts, unit_parts = (
            lax.optimization_barrier(
                (moving, row, out_sends, first_full, ln1_parts, normed_parts, cot_parts, unit_parts)
            )
        )
        if both is not None:
            both, travel, second, row = lax.optimization_barrier((both, travel, second, row))
        here = places[s * y_count : (s + 1) * y_count]
        first_full = assemble(first_full, row, here, first_cuts)
        out_sends.append(jnp.stack([b[:, 3 * unit :] for b in row]))
    full_qkv, col_out = first_full

    second_cuts = [lambda b: b[0], lambda b: b[1]]
    second_row = along_y(travel)
    travel = ring_z(travel)
    out_sends.append(ctx_swap(out_sends.pop(), top))

    ids = jnp.stack([c, lax.axis_index("dp")]).astype(jnp.int32)
    seg_blocks = seg_row.reshape(ctx, rows)
    seg = jnp.concatenate([pick(seg_blocks, c ^ r) for r in order]).astype(F32)
    pos = jnp.concatenate([(c ^ r) * rows + jnp.arange(rows, dtype=jnp.int32) for r in order])
    tokens_row = jnp.stack([pos.astype(F32), seg])
    tokens_col = tokens_row.T
    slopes = jnp.exp2(-8.0 * (c * heads + 1 + jnp.arange(heads)).astype(F32) / HEADS)

    ln1_all, qkv_heads, attn_heads, lse, attn_near, attn_far = attention_forward(
        ids, slopes, ln1_parts, full_qkv, qv_bias.reshape(2 * ctx, unit), tokens_col, tokens_row, unit
    )

    def heads_joined(got):
        return jnp.concatenate([got[r] for r in order], axis=0)

    second_full = assemble(None, second, places[:y_count], second_cuts)
    attn_near, attn_far, travel, second_row, out_sends, second_full = lax.optimization_barrier(
        (attn_near, attn_far, travel, second_row, out_sends, second_full)
    )
    pieces = trade(attn_near, attn_far)
    second_full = assemble(second_full, second_row, places[y_count : 2 * y_count], second_cuts)
    second_row = along_y(travel)
    travel = ring_z(travel)
    (out_got,) = assemble(
        None, [g[t] for g in out_sends for t in range(y_count)], places, [lambda b: b[...]]
    )
    out_parts = [col_out, out_got]
    for bit in lower:
        out_parts = gather_step(out_parts, bit)
        cot_parts = gather_step(cot_parts, bit)
    out_parts = [out_parts[slots[r]] for r in range(ctx)]
    attn, middle, normed2, inv_std2, ln2_act = project_out(
        ids, pieces, out_parts, stream, out_bias, ln2_gain, ln2_bias
    )
    ln2_parts = gather_step([ln2_act], top)
    ln2_parts, cot_parts, travel, second_row, second_full = lax.optimization_barrier(
        (ln2_parts, cot_parts, travel, second_row, second_full)
    )
    second_full = assemble(second_full, second_row, places[2 * y_count : 3 * y_count], second_cuts)
    if (z_count, y_count) == (4, 2):
        got = [travel, jnp.stack([ring_y(travel[0]), ring_z(second_row[1][1])])]
    else:
        got = along_y(travel)
    for bit in lower:
        ln2_parts = gather_step(ln2_parts, bit)
    full_up, full_down = assemble(second_full, got, places[3 * y_count :], second_cuts)
    full_up = full_up.reshape(width, dps * sub)
    unit_bias = pick(jnp.moveaxis(up_bias.reshape(dps, ctx, sub), 1, 0), c).reshape(1, dps * sub)
    ln2_all, cot_all, hidden, slope, *grad_down = feed_forward_hidden(
        ids, ln2_parts, full_up, unit_bias, cot_parts, dps
    )
    pre_bf, up_bias_part, ln2_keep, ln2_send = feed_forward_grad(
        ids, slope, full_up, cot_all, full_down
    )
    ln2_keep, ln2_send = scatter_first(ln2_keep, ln2_send)
    ln2_keep, ln2_got = scatter_rest(ln2_keep, ln2_send)
    grad_up = weight_blocks(ids, ln2_all, pre_bf, dps, 2, earlier=[ln2_send])

    down, up = Reduction(grad_down), Reduction(grad_up)
    down_sent = down.step()
    middle_grad, sums2, grad_near, grad_far, col_near, col_far = middle_backward(
        ids,
        ln2_keep,
        ln2_got,
        normed2,
        inv_std2,
        ln2_gain,
        upstream,
        out_parts,
        earlier=[grad_up[0]],
    )
    grad_pieces = trade(grad_near, grad_far)
    cols = trade(*lax.optimization_barrier((col_near, col_far, grad_pieces[2][0]))[:2])
    qkv_bf, qkv_sums, *kinds = attention_backward(
        ids,
        slopes,
        qkv_heads,
        attn_heads,
        grad_pieces,
        lse,
        tokens_col,
        tokens_row,
        unit,
        earlier=[down_sent, down.terms[1][0]],
    )
    cols_got, qkv_bf, *kinds = lax.optimization_barrier(
        ([a for a, _ in cols], qkv_bf, *kinds)
    )
    cols = [(a, i) for a, (_, i) in zip(cols_got, cols)]
    kinds = unit_columns_home(kinds, c)
    ln1_keep, ln1_send, small = input_terms(
        ids, qkv_bf, full_qkv, normed_parts, qkv_sums, sums2, up_bias_part, sub
    )
    while down.bits:
        down.step(ln1_send)
    up.step(ln1_send)
    for bit in reversed(lower):
        small = small + ctx_swap(small, bit)
    ln1_keep, ln1_send = scatter_first(ln1_keep, ln1_send)

    ln1_keep, ln1_send, small, kinds = sync([], ln1_keep, ln1_send, small, kinds)
    qkv = Reduction(unit_blocks(ids, ln1_all, kinds, dps))
    ln1_keep, ln1_got = scatter_rest(ln1_keep, ln1_send)
    small_got = ctx_swap(small, top)

    ln1_got, small_got = sync([down, up], ln1_got, small_got)
    small = small + small_got
    bits = dp_bits()
    small_got = dp_swap(small, bits[0])
    attn_parts = gather_step([attn], top)
    while up.bits:
        up.step()
    input_grad = input_backward(ln1_keep, ln1_got, normed1, inv_std1, ln1_gain, middle_grad)
    result_keep, result_send = scatter_first(*times_weight(hidden, full_down, earlier=[ln1_got]))
    down_home = trade(*down.result(piece_shapes(ctx, sub, unit), column_pieces(ctx)))

    attn_parts, small_got, result_keep, result_send, down_got = sync(
        [up, qkv], attn_parts, small_got, result_keep, result_send, [a for a, _ in down_home]
    )
    down_home = [(a, i) for a, (_, i) in zip(down_got, down_home)]
    qkv.step()
    small = small + small_got
    small_got = dp_swap(small, bits[1])
    for bit in lower:
        attn_parts = gather_step(attn_parts, bit)
    grad_out = out_blocks(ids, attn_parts, cols, dps)
    out = Reduction(grad_out)
    result_keep, result_got = scatter_rest(result_keep, result_send)
    up_rows = w_up.shape[0]
    up_out = up.result(piece_shapes(ctx, up_rows, dps * sub // ctx), column_pieces(ctx))
    up_home = trade(*up_out)

    up_got, result_got = sync([qkv], [a for a, _ in up_home], result_got)
    up_home = [(a, i) for a, (_, i) in zip(up_got, up_home)]
    while qkv.bits:
        qkv.step()
    out.step()
    shard_up, shard_down = units_home(
        ids, up_home, down_home, w_up.shape, w_down.shape, sub
    )
    result = add_result(middle, result_keep, result_got, down_bias)

    small_got, shard_up, shard_down, result = sync([qkv, out], small_got, shard_up, shard_down, result)
    shard_qkv = qkv.result([(w_qkv.shape, F32)], store_block)[0]
    while out.bits:
        out.step()
    small = small + small_got
    for bit in bits[2:]:
        small = small + dp_swap(small, bit)
    sum_out = out.result([((up_rows, unit), F32)], store_block)[0]

    return (
        result[None],
        input_grad[None],
        small[0],
        small[1],
        shard_qkv,
        small[2:4].reshape(2 * width),
        sum_out,
        small[4],
        small[5],
        small[6],
        shard_up,
        small[8:].reshape(ff),
        shard_down,
        small[7],
    )


def solution(mesh):
    tokens = P("dp", "ctx", None)
    weight = P("dp", "ctx")
    placed = (
        tokens,
        P("dp", None),
        P(),
        P(),
        weight,
        P(),
        weight,
        P(),
        P(),
        P(),
        weight,
        P(),
        weight,
        P(),
        tokens,
    )
    return jax.shard_map(
        per_device,
        mesh=mesh,
        in_specs=placed,
        out_specs=(
            tokens,
            tokens,
            P(),
            P(),
            weight,
            P(),
            weight,
            P(),
            P(),
            P(),
            weight,
            P(),
            weight,
            P(),
        ),
        check_vma=False,
    )
```

```python
import math

import jax
import jax.numpy as jnp
from jax import lax
from jax.experimental import pallas as pl
from jax.experimental.pallas import tpu as pltpu
from jax.sharding import PartitionSpec as P

HEADS = 16
HEAD_DIM = 64

epsilon = 1e-05
gelu_scale = 0.7978845608028654
cubic_term = 0.044715
neg_large = -1e30
BF = jnp.bfloat16
F32 = jnp.float32


def layer_norm(values, gain, offset):
    center = jnp.mean(values, axis=-1, keepdims=True)
    centered = values - center
    variance = jnp.mean(centered * centered, axis=-1, keepdims=True)
    inv_std = lax.rsqrt(variance + epsilon)
    normed = centered * inv_std
    return (normed * gain + offset, normed, inv_std)


def norm_backward(upstream, normed, inv_std, gain):
    scaled = upstream * gain
    return inv_std * (
        scaled
        - jnp.mean(scaled, axis=-1, keepdims=True)
        - normed * jnp.mean(scaled * normed, axis=-1, keepdims=True)
    )


def gelu_both(values):
    square = values * values
    tangent = jnp.tanh(gelu_scale * (values + cubic_term * values * square))
    forward = 0.5 * values * (1.0 + tangent)
    slope = 0.5 * (1.0 + tangent) + 0.5 * values * (1.0 - tangent * tangent) * gelu_scale * (
        1.0 + 3.0 * cubic_term * square
    )
    return forward, slope


def dot(a, b):
    return jnp.dot(a, b, preferred_element_type=F32)


def dot_nt(a, b):
    return lax.dot_general(a, b, (((1,), (1,)), ((), ())), preferred_element_type=F32)


def dot_tn(a, b):
    return lax.dot_general(a, b, (((0,), (0,)), ((), ())), preferred_element_type=F32)


def pick(stack, index):
    return lax.dynamic_index_in_dim(stack, index, 0, keepdims=False)


def ctx_bits(count):
    bits = []
    bit = count // 2
    while bit:
        bits.append(bit)
        bit //= 2
    return bits


def ctx_order(count):
    order = [0]
    for bit in ctx_bits(count):
        order = order + [r | bit for r in order]
    return order


def ctx_swap(x, bit):
    count = lax.axis_size("ctx")
    return lax.ppermute(x, "ctx", [(i, i ^ bit) for i in range(count)])


def gather_step(pieces, bit):
    return pieces + [ctx_swap(p, bit) for p in pieces]


def ctx_gather(x):
    pieces = [x]
    for bit in ctx_bits(lax.axis_size("ctx")):
        pieces = gather_step(pieces, bit)
    return jnp.concatenate(pieces, axis=0)


def ctx_scatter(x):
    for bit in reversed(ctx_bits(lax.axis_size("ctx"))):
        half = x.shape[0] // 2
        x = x[:half] + ctx_swap(x[half:].astype(BF), bit).astype(F32)
    return x


def exchange_step(pieces, bit):
    pieces = list(pieces)
    slots = [r for r in range(len(pieces)) if r & bit]
    got = ctx_swap(jnp.stack([pieces[r] for r in slots]), bit)
    for i, r in enumerate(slots):
        pieces[r] = got[i]
    return pieces


def ctx_exchange(pieces):
    for bit in ctx_bits(lax.axis_size("ctx")):
        pieces = exchange_step(pieces, bit)
    return pieces


def trade(near, far, *earlier):
    count = 2 * near.shape[0]
    if count == 4:
        got = ctx_swap(far, 2)
        if earlier:
            got = after(got, *earlier)
        return [(near, 0), (ctx_swap(near, 1), 1), (got, 0), (ctx_swap(got, 1), 1)]
    pieces = ctx_exchange([*near, *far])
    return [(piece[None], 0) for piece in pieces]


def put_piece(near_ref, far_ref, r, value):
    half = near_ref.shape[0]
    (near_ref if r < half else far_ref)[r % half] = value


def put_piece_at(near_ref, far_ref, slot, value):
    half = near_ref.shape[0]

    @pl.when(slot < half)
    def _():
        near_ref[slot] = value

    @pl.when(slot >= half)
    def _():
        far_ref[slot - half] = value


def piece_shapes(ctx, rows, width):
    return [((ctx // 2, rows, width), BF)] * 2


def owned(ids, pieces, k):
    value = pieces[0]
    for r in range(1, len(pieces)):
        value = jnp.where(ids[0] == (k ^ r), pieces[r], value)
    return value


def by_owner(pieces, me, axis):
    stack = jnp.stack(pieces)
    return jnp.concatenate([pick(stack, me ^ k) for k in range(len(pieces))], axis=axis)


def dp_shape(count):
    z_count = 4 if count % 4 == 0 else count
    return z_count, count // z_count


def ring_z(x):
    count = lax.axis_size("dp")
    _, y_count = dp_shape(count)
    return lax.ppermute(x, "dp", [(i, (i + y_count) % count) for i in range(count)])


def ring_y(x):
    count = lax.axis_size("dp")
    _, y_count = dp_shape(count)
    return lax.ppermute(
        x, "dp", [(i, i // y_count * y_count + (i + 1) % y_count) for i in range(count)]
    )


def along_y(x):
    row = [x]
    for _ in range(dp_shape(lax.axis_size("dp"))[1] - 1):
        row.append(ring_y(row[-1]))
    return row


def dp_places(reverse=False):
    count = lax.axis_size("dp")
    z_count, y_count = dp_shape(count)
    me = lax.axis_index("dp")
    z, y = me // y_count, me % y_count
    places = []
    for s in range(z_count):
        for t in range(y_count):
            places.append((z + z_count - s) % z_count * y_count + (y + y_count - t) % y_count)
    return places


def after(x, *earlier):
    return lax.optimization_barrier((x, *earlier))[0]


def call(kernel, outs, args, scalars=1, scratch=(), work=0, earlier=(), far=()):
    used = len(args)
    sizes = [(x.shape, x.dtype) for x in args] + list(outs) + [(x.shape, x.dtype) for x in scratch]
    held = sum(math.prod(shape) * jnp.dtype(dtype).itemsize for shape, dtype in sizes)
    limit = held * 5 // 4 + work + 4 * 2**20
    first_out = used + len(earlier)
    fetched = [pltpu.VMEM(args[i].shape, args[i].dtype) for i in far]
    if far:
        fetched.append(pltpu.SemaphoreType.DMA((len(far),)))

    def body(*refs):
        ins, rest = list(refs[:used]), refs[first_out:]
        if far:
            rest, buffers, sem = rest[: -len(far) - 1], rest[-len(far) - 1 : -1], rest[-1]
            copies = [
                pltpu.make_async_copy(ins[i], buffer, sem.at[j])
                for j, (i, buffer) in enumerate(zip(far, buffers))
            ]
            for copy in copies:
                copy.start()
            for copy in copies:
                copy.wait()
            for i, buffer in zip(far, buffers):
                ins[i] = buffer
        kernel(*ins, *rest)

    def space(i):
        if i in far:
            return pltpu.HBM
        return pltpu.SMEM if i < scalars else pl.ANY if i >= used else pltpu.VMEM

    return pl.pallas_call(
        body,
        out_shape=[jax.ShapeDtypeStruct(shape, dtype) for shape, dtype in outs],
        in_specs=[pl.BlockSpec(memory_space=space(i)) for i in range(first_out)],
        out_specs=[pl.BlockSpec(memory_space=pltpu.VMEM)] * len(outs),
        scratch_shapes=[*scratch, *fetched],
        compiler_params=pltpu.CompilerParams(vmem_limit_bytes=limit),
    )(*args, *earlier)


def assemble(full, blocks, places, cuts):
    count, held = len(blocks), len(cuts)
    shapes = [cut(jnp.zeros(blocks[0].shape, BF)).shape for cut in cuts]
    total = lax.axis_size("dp")

    def kernel(place_ref, *refs):
        outs = refs[-held:]
        for i in range(count):
            for out_ref, cut, (rows, _) in zip(outs, cuts, shapes):
                at = pl.multiple_of(place_ref[i] * rows, rows)
                out_ref[pl.ds(at, rows), :] = cut(refs[i])

    return pl.pallas_call(
        kernel,
        out_shape=[jax.ShapeDtypeStruct((total * rows, width), BF) for rows, width in shapes],
        in_specs=[pl.BlockSpec(memory_space=pltpu.SMEM)]
        + [pl.BlockSpec(memory_space=pltpu.VMEM)] * (count + (held if full else 0)),
        out_specs=[pl.BlockSpec(memory_space=pltpu.VMEM)] * held,
        input_output_aliases={1 + count + j: j for j in range(held)} if full else {},
        compiler_params=pltpu.CompilerParams(
            vmem_limit_bytes=4 * 2**20 + 6 * sum(total * rows * width for rows, width in shapes)
        ),
    )(jnp.stack(places).astype(jnp.int32), *blocks, *(full or []))


def dp_bits():
    bits = []
    bit = 1
    while bit < lax.axis_size("dp"):
        bits.append(bit)
        bit *= 2
    return bits


def slot_order(bits):
    order = [0]
    for bit in reversed(bits):
        order = order + [r | bit for r in order]
    return order


def grad_blocks(ids, left_ref, right, keep_ref, *send_refs):
    half, rows = keep_ref.shape[:2]
    bits = []
    while 2 ** len(bits) < 2 * half:
        bits.append(2 ** len(bits))
    ranges = [(keep_ref, 0)]
    for ref in send_refs[::-1]:
        ranges.append((ref, ranges[-1][1] + ranges[-1][0].shape[0]))
    for k in range(2 * half):
        block = dot_tn(left_ref[:, k * rows : (k + 1) * rows], right).astype(BF)
        name = jnp.bitwise_xor(ids[1], k)
        slot = 0
        for i, bit in enumerate(bits):
            slot = slot + lax.div(jnp.bitwise_and(name, bit), bit) * (half >> i)
        for ref, first in ranges:

            @pl.when((slot >= first) & (slot < first + ref.shape[0]))
            def _():
                ref[slot - first] = block


def block_shapes(dps, rows, width, parts):
    half = dps // 2
    counts = [half] + ([half] if parts == 1 else [half - half // 2, half // 2])
    return [((n, rows, width), BF) for n in counts]


def dp_swap(x, bit):
    count = lax.axis_size("dp")
    return lax.ppermute(x, "dp", [(i, i ^ bit) for i in range(count)])


def combine(terms, start, count, outs, write, earlier=()):

    def kernel(ids, *refs):
        for i in range(count):
            total = refs[0][start - terms[0][1] + i].astype(F32)
            for ref, (_, first) in zip(refs[1 : len(terms)], terms[1:]):
                total = total + ref[start - first + i].astype(F32)
            write(ids, i, total, refs[len(terms) :])

    ids = lax.axis_index("ctx").astype(jnp.int32)[None]
    return call(kernel, outs, [ids] + [array for array, _ in terms], earlier=earlier)


class Reduction:

    def __init__(self, blocks):
        keep, *sends = blocks
        self.bits = dp_bits()
        self.size = keep.shape[0]
        bit = self.bits.pop(0)
        got = [dp_swap(send, bit) for send in sends]
        self.first = [(keep, 0), (got[0], self.size - got[0].shape[0])]
        self.terms = [(keep, 0), (got[-1], 0)]

    def step(self, *earlier):
        self.size //= 2
        terms, self.first = self.first or self.terms, None
        last = len(self.bits) == 1

        def write(ids, i, block, refs):
            refs[0][i] = block.astype(BF)

        def write_both(ids, i, block, refs):
            if i:
                refs[0][0] = block.astype(BF)
            else:
                refs[1][0] = block

        block = terms[0][0].shape[1:]
        if last and terms is self.terms:
            outs = [((1,) + block, BF), ((1,) + block, F32)]
            send, own = combine(terms, 0, 2, outs, write_both, earlier)
            self.terms = [(own, 0)]
        else:
            outs = [((self.size,) + block, BF)]
            (send,) = combine(terms, self.size, self.size, outs, write, earlier)
        self.terms.append((dp_swap(send, self.bits.pop(0)), 0))
        return send

    def result(self, outs, write, *earlier):
        return combine(self.terms, 0, 1, outs, write, earlier)


def sync(reductions, *values):
    held = [([a for a, _ in r.first or []], [a for a, _ in r.terms]) for r in reductions]
    held, values = lax.optimization_barrier((held, values))
    for r, (first, terms) in zip(reductions, held):
        if r.first:
            r.first = [(a, at) for a, (_, at) in zip(first, r.first)]
        r.terms = [(a, at) for a, (_, at) in zip(terms, r.terms)]
    return values


def unit_pieces(w_up, w_down, c, sub, unit):
    ctx, dps = lax.axis_size("ctx"), lax.axis_size("dp")
    down_view = w_down.reshape(ctx, sub, unit)
    up_view = jnp.moveaxis(w_up.reshape(w_up.shape[0], dps // ctx, ctx, sub), 2, 0).reshape(
        ctx, sub, unit
    )
    return [jnp.stack([pick(up_view, c ^ r), pick(down_view, c ^ r)]) for r in range(ctx)]


def join_units(pieces, c, up_rows):
    unit_up = by_owner([p[0].reshape(up_rows, -1) for p in pieces], c, 1)
    unit_down = by_owner([p[1] for p in pieces], c, 1)
    return jnp.stack([unit_up.reshape(unit_down.shape), unit_down])


def store_block(ids, i, block, refs):
    refs[0][...] = block


def column_pieces(ctx):

    def write(ids, i, block, refs):
        part = block.shape[1] // ctx
        for k in range(ctx):
            value = block[:, k * part : (k + 1) * part].astype(BF)
            put_piece_at(*refs, jnp.bitwise_xor(ids[0], k), value)

    return write


def units_home(ids, up_pieces, down_pieces, up_shape, down_shape, sub, earlier=()):
    ctx = len(up_pieces)

    def kernel(ids, *refs):
        up_ref, down_ref = refs[2 * ctx :]
        ups = [ref[i] for ref, (_, i) in zip(refs, up_pieces)]
        downs = [ref[i] for ref, (_, i) in zip(refs[ctx:], down_pieces)]
        for k in range(ctx):
            down_ref[k * sub : (k + 1) * sub, :] = owned(ids, downs, k).astype(F32)
            value = owned(ids, ups, k).astype(F32)
            for i in range(value.shape[1] // sub):
                at = (i * ctx + k) * sub
                up_ref[:, at : at + sub] = value[:, i * sub : (i + 1) * sub]

    return call(
        kernel,
        [(up_shape, F32), (down_shape, F32)],
        [ids] + [array for array, _ in up_pieces + down_pieces],
        earlier=earlier,
    )


def add_result(middle, keep, got, bias, earlier=()):

    def kernel(ids, middle_ref, keep_ref, got_ref, bias_ref, out_ref):
        out_ref[...] = middle_ref[...] + keep_ref[...] + got_ref[...].astype(F32) + bias_ref[...]

    return call(
        kernel,
        [(middle.shape, F32)],
        [jnp.zeros((1,), jnp.int32), middle, keep, got, bias[None]],
        earlier=earlier,
    )[0]


def ctx_sum(x):
    for bit in reversed(ctx_bits(lax.axis_size("ctx"))):
        x = x + ctx_swap(x, bit)
    return x


def score_tile(q, k, slope, gap):
    return dot_nt(q, k) * (1.0 / math.sqrt(HEAD_DIM)) - slope * gap


def pair_gaps(pos_q, pos_k, seg_q, seg_k):
    allowed = (pos_k <= pos_q) & (seg_k == seg_q)
    return jnp.where(allowed, pos_q - pos_k, jnp.inf)


def attention_forward(ids, slopes, ln1_parts, full_qkv, qv_rows, tokens_col, tokens_row, unit):
    rows, width = ln1_parts[0].shape
    seq = rows * len(ln1_parts)
    tile = min(seq, 512)
    heads = unit // HEAD_DIM
    ctx = qv_rows.shape[0] // 2

    order = ctx_order(ctx)

    def kernel(ids, slopes, w_ref, bias_ref, col_ref, row_ref, *refs):
        x_ref, qkv_ref, attn_ref, lse_ref, near_ref, far_ref = refs[ctx:]
        for i in range(ctx):
            x_ref[i * rows : (i + 1) * rows, :] = refs[i][...]
        q_bias = bias_ref[pl.ds(ids[0], 1), :]
        v_bias = bias_ref[pl.ds(ctx + ids[0], 1), :]
        x = x_ref[...]
        qkv_ref[:, :unit] = (dot(x, w_ref[:, :unit]) + q_bias).astype(BF)
        qkv_ref[:, unit : 2 * unit] = dot(x, w_ref[:, unit : 2 * unit]).astype(BF)
        qkv_ref[:, 2 * unit :] = (dot(x, w_ref[:, 2 * unit :]) + v_bias).astype(BF)
        for lo in range(0, seq, tile):
            at = slice(lo, lo + tile)
            gap = pair_gaps(
                col_ref[at, 0:1], row_ref[0:1, :], col_ref[at, 1:2], row_ref[1:2, :]
            )
            for h in range(heads):
                cols = [slice(j * unit + h * HEAD_DIM, j * unit + (h + 1) * HEAD_DIM) for j in range(3)]
                scores = score_tile(qkv_ref[at, cols[0]], qkv_ref[:, cols[1]], slopes[h], gap)
                row_max = jnp.max(scores, axis=-1, keepdims=True)
                probs = jnp.exp(scores - row_max)
                row_sum = jnp.sum(probs, axis=-1, keepdims=True)
                out = dot(probs.astype(BF), qkv_ref[:, cols[2]]) / row_sum
                attn_ref[at, cols[0]] = out.astype(BF)
                lse_ref[at, h : h + 1] = row_max + jnp.log(row_sum)
        for i, r in enumerate(order):
            put_piece(near_ref, far_ref, r, attn_ref[i * rows : (i + 1) * rows, :])

    return call(
        kernel,
        [((seq, width), BF), ((seq, 3 * unit), BF), ((seq, unit), BF), ((seq, heads), F32)]
        + piece_shapes(ctx, rows, unit),
        [ids, slopes, full_qkv, qv_rows, tokens_col, tokens_row, *ln1_parts],
        scalars=2,
        work=20 * tile * seq,
    )


def attention_backward(
    ids, slopes, qkv, attn, pieces, lse, tokens_col, tokens_row, unit, earlier=()
):
    seq = qkv.shape[0]
    ctx = len(pieces)
    order = ctx_order(ctx)
    rows = seq // ctx
    tile = min(seq, 512)
    heads = unit // HEAD_DIM
    inv_root = 1.0 / math.sqrt(HEAD_DIM)

    def kernel(ids, slopes, qkv_ref, attn_ref, lse_ref, col_ref, row_ref, *refs):
        out_ref, sum_ref, *kind_refs, total_ref, grad_ref = refs[ctx:]
        for i, r in enumerate(order):
            grad_ref[i * rows : (i + 1) * rows, :] = refs[r][pieces[r][1]]
        for lo in range(0, seq, tile):
            at = slice(lo, lo + tile)
            gap = pair_gaps(
                col_ref[at, 0:1], row_ref[0:1, :], col_ref[at, 1:2], row_ref[1:2, :]
            )
            for h in range(heads):
                cols = [slice(j * unit + h * HEAD_DIM, j * unit + (h + 1) * HEAD_DIM) for j in range(3)]
                q, k, v = qkv_ref[at, cols[0]], qkv_ref[:, cols[1]], qkv_ref[:, cols[2]]
                do = grad_ref[at, cols[0]]
                delta = jnp.sum(
                    do.astype(F32) * attn_ref[at, cols[0]].astype(F32), axis=-1, keepdims=True
                )
                probs = jnp.exp(score_tile(q, k, slopes[h], gap) - lse_ref[at, h : h + 1])
                score_bf = (probs * (dot_nt(do, v) - delta)).astype(BF)
                total_ref[at, cols[0]] = inv_root * dot(score_bf, k)
                dk = inv_root * dot_tn(score_bf, q)
                dv = dot_tn(probs.astype(BF), do)
                if lo:
                    dk = dk + total_ref[:, cols[1]]
                    dv = dv + total_ref[:, cols[2]]
                total_ref[:, cols[1]] = dk
                total_ref[:, cols[2]] = dv
        total = total_ref[...]
        out_ref[...] = total.astype(BF)
        sum_ref[...] = jnp.sum(total, axis=0, keepdims=True)
        for j in range(3):
            slot = j
            if ctx == 4 and j != 1:
                slot = jnp.where(lax.rem(ids[0], 2) == 0, j, 2 - j)
            kind = lax.rem((slot + 3 * ctx - ids[0]) * ctx, 3)
            value = out_ref[:, :unit]
            for k in range(1, 3):
                value = jnp.where(kind == k, out_ref[:, k * unit : (k + 1) * unit], value)
            kind_refs[j][...] = value

    return call(
        kernel,
        [((seq, 3 * unit), BF), ((1, 3 * unit), F32)] + [((seq, unit), BF)] * 3,
        [ids, slopes, qkv, attn, lse, tokens_col, tokens_row]
        + [array for array, _ in pieces],
        scalars=2,
        work=28 * tile * seq,
        scratch=[pltpu.VMEM((seq, 3 * unit), F32), pltpu.VMEM((seq, unit), BF)],
        earlier=earlier,
    )


def split_halves(value, keep_ref, send_ref):
    half = keep_ref.shape[0]
    keep_ref[...] = value[:half]
    send_ref[...] = value[half:].astype(BF)


def input_terms(ids, x, weight, normed_parts, qkv_sums, sums2, up_sums, sub):
    rows, width = x.shape[0], weight.shape[0]
    ctx = len(normed_parts)
    unit = width // ctx
    part = rows // ctx
    units = up_sums.shape[1]
    small_rows = 8 + units * ctx // width

    def kernel(ids, x_ref, w_ref, qkv_ref, sums_ref, up_ref, *refs):
        normed_refs = refs[:ctx]
        keep_ref, send_ref, small_ref = refs[ctx:]
        terms = dot_nt(x_ref[...], w_ref[...])
        split_halves(terms, keep_ref, send_ref)
        gain = jnp.zeros((1, width), F32)
        for i in range(ctx):
            product = terms[i * part : (i + 1) * part] * normed_refs[i][...].astype(F32)
            gain = gain + jnp.sum(product, axis=0, keepdims=True)
        small_ref[0:1, :] = gain
        small_ref[1:2, :] = jnp.sum(terms, axis=0, keepdims=True)
        small_ref[4:5, :] = sums_ref[2:3, :]
        small_ref[5:6, :] = sums_ref[0:1, :]
        small_ref[6:7, :] = sums_ref[1:2, :]
        small_ref[7:8, :] = sums_ref[3:4, :]
        for k in range(ctx):
            mine = ids[0] == k
            at = slice(k * unit, (k + 1) * unit)
            small_ref[2:3, at] = jnp.where(mine, qkv_ref[:, :unit], 0.0)
            small_ref[3:4, at] = jnp.where(mine, qkv_ref[:, 2 * unit :], 0.0)
            for j in range(units // sub):
                row, col = divmod((j * ctx + k) * sub, width)
                value = jnp.where(mine, up_ref[:, j * sub : (j + 1) * sub], 0.0)
                small_ref[8 + row : 9 + row, col : col + sub] = value

    return call(
        kernel,
        [((rows // 2, width), F32), ((rows // 2, width), BF), ((small_rows, width), F32)],
        [ids, x, weight, qkv_sums, sums2, up_sums, *normed_parts],
        work=8 * rows * width,
    )


def feed_forward_hidden(ids, ln2_parts, full_up, unit_bias, cot_parts, dps, earlier=()):
    ctx = len(ln2_parts)
    rows, width = ln2_parts[0].shape
    seq = rows * ctx
    units = full_up.shape[1]

    def kernel(ids, up_ref, bias_ref, *refs):
        x_ref, cot_ref, hidden_ref, slope_ref, *block_refs = refs[2 * ctx :]
        for i in range(ctx):
            x_ref[i * rows : (i + 1) * rows, :] = refs[i][...]
            cot_ref[i * rows : (i + 1) * rows, :] = refs[ctx + i][...]
        forward, slope = gelu_both(dot(x_ref[...], up_ref[...]) + bias_ref[...])
        slope_ref[...] = slope
        hidden_ref[...] = forward.astype(BF)
        grad_blocks(ids, hidden_ref, cot_ref[...], *block_refs)

    return call(
        kernel,
        [((seq, width), BF), ((seq, width), BF), ((seq, units), BF), ((seq, units), F32)]
        + block_shapes(dps, units // dps, width, 2),
        [ids, full_up, unit_bias, *ln2_parts, *cot_parts],
        work=16 * seq * units,
        earlier=earlier,
    )


def feed_forward_grad(ids, slope, full_up, cot_all, full_down):
    seq, units = slope.shape
    width = cot_all.shape[1]

    def kernel(ids, slope_ref, up_ref, cot_ref, down_ref, pre_ref, sum_ref, keep_ref, send_ref):
        pre_grad = dot_nt(cot_ref[...], down_ref[...]) * slope_ref[...]
        sum_ref[...] = jnp.sum(pre_grad, axis=0, keepdims=True)
        pre_ref[...] = pre_grad.astype(BF)
        split_halves(dot_nt(pre_ref[...], up_ref[...]), keep_ref, send_ref)

    return call(
        kernel,
        [
            ((seq, units), BF),
            ((1, units), F32),
            ((seq // 2, width), F32),
            ((seq // 2, width), BF),
        ],
        [ids, slope, full_up, cot_all, full_down],
        work=12 * seq * units,
    )


def weight_blocks(ids, left, right, dps, parts, earlier=()):

    def kernel(ids, left_ref, right_ref, *block_refs):
        grad_blocks(ids, left_ref, right_ref[...], *block_refs)

    shapes = block_shapes(dps, left.shape[1] // dps, right.shape[1], parts)
    return call(kernel, shapes, [ids, left, right], earlier=earlier)


def out_blocks(ids, attn_parts, cols, dps, earlier=()):
    ctx = len(cols)
    order = ctx_order(ctx)
    rows, width = attn_parts[0].shape
    unit = cols[0][0].shape[2]

    def kernel(ids, *refs):
        *block_refs, left_ref, right_ref = refs[2 * ctx :]
        for i, r in enumerate(order):
            at = slice(i * rows, (i + 1) * rows)
            left_ref[at, :] = refs[i][...]
            right_ref[at, :] = refs[ctx + r][cols[r][1]]
        grad_blocks(ids, left_ref, right_ref[...], *block_refs)

    return call(
        kernel,
        block_shapes(dps, width // dps, unit, 1),
        [ids, *attn_parts] + [array for array, _ in cols],
        scratch=[pltpu.VMEM((ctx * rows, width), BF), pltpu.VMEM((ctx * rows, unit), BF)],
        earlier=earlier,
    )


def unit_blocks(ids, left, kinds, dps):
    seq, width = left.shape
    unit = kinds[0].shape[1]
    ctx = width // unit
    rows = seq // ctx
    bits = ctx_bits(ctx)

    def kernel(ids, left_ref, *refs):
        kind_refs, block_refs, right_ref = refs[:3], refs[3:-1], refs[-1]
        if ctx == 4:
            even = lax.rem(ids[0], 2) == 0
            for i in range(ctx):
                at = slice(i * rows, (i + 1) * rows)
                stayed = kind_refs[0][at, :]
                crossed = kind_refs[2][(i ^ 1) * rows : ((i ^ 1) + 1) * rows, :]
                right_ref[at, :unit] = jnp.where(even, stayed, crossed)
                right_ref[at, unit : 2 * unit] = kind_refs[1][
                    (i ^ 2) * rows : ((i ^ 2) + 1) * rows, :
                ]
                right_ref[at, 2 * unit :] = jnp.where(even, crossed, stayed)
        for j in range(3 if ctx != 4 else 0):
            apart = jnp.bitwise_xor(ids[0], lax.rem(3 * ids[0] + j, ctx))
            shift = 0
            for i, bit in enumerate(bits):
                shift = shift + lax.div(jnp.bitwise_and(apart, bit), bit) * (1 << i)
            for i in range(ctx):
                at = pl.multiple_of(jnp.bitwise_xor(shift, i) * rows, rows)
                right_ref[i * rows : (i + 1) * rows, j * unit : (j + 1) * unit] = kind_refs[j][
                    pl.ds(at, rows), :
                ]
        grad_blocks(ids, left_ref, right_ref[...], *block_refs)

    return call(
        kernel,
        block_shapes(dps, width // dps, 3 * unit, 1),
        [ids, left, *kinds],
        scratch=[pltpu.VMEM((seq, 3 * unit), BF)],
    )


def unit_columns_home(slots, c):
    ctx = lax.axis_size("ctx")
    if ctx != 4:
        return [
            lax.ppermute(slots[j], "ctx", [((3 * i + j) % ctx, i) for i in range(ctx)])
            for j in range(3)
        ]
    return [slots[0], ctx_swap(slots[1], 1), ctx_swap(slots[2], 2)]


def times_weight(x, weight, earlier=()):
    rows, width = x.shape[0], weight.shape[1]

    def kernel(ids, x_ref, w_ref, keep_ref, send_ref):
        split_halves(dot(x_ref[...], w_ref[...]), keep_ref, send_ref)

    return call(
        kernel,
        [((rows // 2, width), F32), ((rows // 2, width), BF)],
        [jnp.zeros((1,), jnp.int32), x, weight],
        earlier=earlier,
    )


def scatter_step(keep, got, earlier=()):
    rows, width = keep.shape

    def kernel(ids, keep_ref, got_ref, next_ref, send_ref):
        split_halves(keep_ref[...] + got_ref[...].astype(F32), next_ref, send_ref)

    return call(
        kernel,
        [((rows // 2, width), F32), ((rows // 2, width), BF)],
        [jnp.zeros((1,), jnp.int32), keep, got],
        earlier=earlier,
    )


def scatter_first(keep, send, earlier=()):
    for bit in list(reversed(ctx_bits(lax.axis_size("ctx"))))[:-1]:
        keep, send = scatter_step(keep, ctx_swap(send, bit), earlier)
    return keep, send


def scatter_rest(keep, send):
    return keep, ctx_swap(send, lax.axis_size("ctx") // 2)


def project_out(ids, pieces, out_parts, stream, out_bias, gain, offset):
    _, rows, unit = pieces[0][0].shape
    ctx = len(pieces)
    width = stream.shape[1]

    def kernel(ids, *refs):
        piece_refs, w_refs = refs[:ctx], refs[ctx : 2 * ctx]
        stream_ref, bias_ref, gain_ref, offset_ref = refs[2 * ctx : 2 * ctx + 4]
        attn_ref, middle_ref, normed_ref, inv_ref, act_ref = refs[2 * ctx + 4 :]
        got = [ref[i] for ref, (_, i) in zip(piece_refs, pieces)]
        for k in range(ctx):
            attn_ref[:, k * unit : (k + 1) * unit] = owned(ids, got, k)
        parts = [dot(attn_ref[...], w_refs[r][...]) for r in range(ctx)]
        for k in range(ctx):
            at = slice(k * unit, (k + 1) * unit)
            middle_ref[:, at] = stream_ref[:, at] + owned(ids, parts, k) + bias_ref[:, at]
        out, normed, inv_std = layer_norm(middle_ref[...], gain_ref[...], offset_ref[...])
        normed_ref[...] = normed
        inv_ref[...] = inv_std
        act_ref[...] = out.astype(BF)

    full = (rows, width)
    return call(
        kernel,
        [(full, BF), (full, F32), (full, F32), ((rows, 1), F32), (full, BF)],
        [ids]
        + [array for array, _ in pieces]
        + [*out_parts, stream, out_bias[None], gain[None], offset[None]],
    )


def middle_backward(ids, keep, got, normed, inv_std, gain, upstream, out_parts, earlier=()):
    rows, width = upstream.shape
    ctx = len(out_parts)
    unit = width // ctx

    def kernel(ids, keep_ref, got_ref, normed_ref, inv_ref, gain_ref, up_ref, *refs):
        w_refs = refs[:ctx]
        middle_ref, sum_ref, attn_near, attn_far, cols_near, cols_far = refs[ctx:]
        cols = []
        out_grad = keep_ref[...] + got_ref[...].astype(F32)
        normed = normed_ref[...]
        middle_grad = up_ref[...] + norm_backward(out_grad, normed, inv_ref[...], gain_ref[...])
        middle_ref[...] = middle_grad
        sum_ref[0:1, :] = jnp.sum(out_grad * normed, axis=0, keepdims=True)
        sum_ref[1:2, :] = jnp.sum(out_grad, axis=0, keepdims=True)
        sum_ref[2:3, :] = jnp.sum(middle_grad, axis=0, keepdims=True)
        sum_ref[3:4, :] = jnp.sum(up_ref[...], axis=0, keepdims=True)
        middle_bf = middle_grad.astype(BF)
        for r in range(ctx):
            owner = jnp.bitwise_xor(ids[0], r)
            value = middle_bf[:, :unit]
            for k in range(1, ctx):
                value = jnp.where(owner == k, middle_bf[:, k * unit : (k + 1) * unit], value)
            cols.append(value)
            put_piece(cols_near, cols_far, r, value)
        for r in range(ctx):
            at = pl.multiple_of(jnp.bitwise_xor(ids[0], r) * unit, unit)
            total = dot_nt(cols[0], w_refs[0][pl.ds(at, unit), :])
            for j in range(1, ctx):
                total = total + dot_nt(cols[j], w_refs[j][pl.ds(at, unit), :])
            put_piece(attn_near, attn_far, r, total.astype(BF))

    return call(
        kernel,
        [((rows, width), F32), ((4, width), F32)] + piece_shapes(ctx, rows, unit) * 2,
        [ids, keep, got, normed, inv_std, gain[None], upstream, *out_parts],
        far=[3, 6] + list(range(7, 7 + ctx)),
        earlier=earlier,
    )


def input_backward(keep, got, normed, inv_std, gain, middle_grad, earlier=()):
    rows, width = middle_grad.shape

    def kernel(ids, keep_ref, got_ref, normed_ref, inv_ref, gain_ref, mid_ref, out_ref):
        out_grad = keep_ref[...] + got_ref[...].astype(F32)
        out_ref[...] = mid_ref[...] + norm_backward(
            out_grad, normed_ref[...], inv_ref[...], gain_ref[...]
        )

    return call(
        kernel,
        [((rows, width), F32)],
        [jnp.zeros((1,), jnp.int32), keep, got, normed, inv_std, gain[None], middle_grad],
        earlier=earlier,
    )[0]


def per_device(
    layer_input,
    segment_ids,
    ln1_gain,
    ln1_bias,
    w_qkv,
    qv_bias,
    w_out,
    out_bias,
    ln2_gain,
    ln2_bias,
    w_up,
    up_bias,
    w_down,
    down_bias,
    cotangent,
):
    stream = layer_input[0]
    upstream = cotangent[0]
    seg_row = segment_ids[0]
    rows, width = stream.shape
    ctx = lax.axis_size("ctx")
    dps = lax.axis_size("dp")
    c = lax.axis_index("ctx")
    seq = rows * ctx
    unit = width // ctx
    heads = HEADS // ctx
    inv_root = 1.0 / math.sqrt(HEAD_DIM)
    ff = up_bias.shape[0]
    sub = ff // dps // ctx
    order = ctx_order(ctx)
    slots = [order.index(r) for r in range(ctx)]
    places = dp_places()

    if ctx == 4:
        odd = c % 2

        def third(at):
            return lax.dynamic_slice_in_dim(w_qkv, at * unit, unit, 1)

        stays = third(2 * odd)
        crossed = ctx_swap(third(2 - 2 * odd), 2)
        beside = ctx_swap(w_qkv[:, unit : 2 * unit], 1)
        three = jnp.stack([stays, crossed, beside])
        held = [(0, 2, 1), (2, 0, 1), (1, 0, 2), (1, 2, 0)]
        place = [
            sum(jnp.where(c == k, held[k][kind], 0) for k in range(4)) for kind in range(3)
        ]
        head_qkv = jnp.concatenate([pick(three, at) for at in place] + [w_out], axis=1)
    else:
        took = [
            lax.ppermute(
                w_qkv[:, j * unit : (j + 1) * unit],
                "ctx",
                [(i, (3 * i + j) % ctx) for i in range(ctx)],
            )
            for j in range(3)
        ]
        took = jnp.stack(took)
        head_qkv = jnp.concatenate(
            [pick(took, (kind * ctx + c) % 3) for kind in range(3)] + [w_out], axis=1
        )

    normed1_out, normed1, inv_std1 = layer_norm(stream, ln1_gain, ln1_bias)
    ln1_act = normed1_out.astype(BF)
    cot_bf = upstream.astype(BF)
    w_up, w_down, ln1_act, cot_bf, normed1 = lax.optimization_barrier(
        (w_up, w_down, ln1_act, cot_bf, normed1, head_qkv)
    )[:5]

    z_count, y_count = dp_shape(dps)
    top, *lower = ctx_bits(ctx)
    first_cuts = [lambda b: b[:, : 3 * unit], lambda b: b[:, 3 * unit :]]
    first_full, out_sends, out_full, second_full = None, [], None, None
    moving = head_qkv
    unit_parts = unit_pieces(w_up, w_down, c, sub, unit)
    ln1_parts = [ln1_act]
    normed_parts = [normed1.astype(BF)]
    cot_parts = [cot_bf]
    both = travel = second = None
    for s in range(z_count):
        last = s == z_count - 1
        row = along_y(moving)
        if not last:
            moving = ring_z(moving)
        if out_sends:
            out_sends.append(ctx_swap(out_sends.pop(), top))
        if s == 0:
            ln1_parts = gather_step(ln1_parts, top)
            unit_parts = exchange_step(unit_parts, top)
        if s == 1 % z_count:
            for bit in lower:
                unit_parts = exchange_step(unit_parts, bit)
            for bit in lower:
                ln1_parts = gather_step(ln1_parts, bit)
            both = join_units(unit_parts, c, w_up.shape[0])
            normed_parts = gather_step(normed_parts, top)
        if s == 2 % z_count:
            for bit in lower:
                normed_parts = gather_step(normed_parts, bit)
        if last:
            cot_parts = gather_step(cot_parts, top)
            second = along_y(both)
            travel = ring_z(both)
        moving, row, out_sends, first_full, ln1_parts, normed_parts, cot_parts, unit_parts = (
            lax.optimization_barrier(
                (moving, row, out_sends, first_full, ln1_parts, normed_parts, cot_parts, unit_parts)
            )
        )
        if both is not None:
            both, travel, second, row = lax.optimization_barrier((both, travel, second, row))
        here = places[s * y_count : (s + 1) * y_count]
        first_full = assemble(first_full, row, here, first_cuts)
        out_sends.append(jnp.stack([b[:, 3 * unit :] for b in row]))
    full_qkv, col_out = first_full

    second_cuts = [lambda b: b[0], lambda b: b[1]]
    second_row = along_y(travel)
    travel = ring_z(travel)
    out_sends.append(ctx_swap(out_sends.pop(), top))

    ids = jnp.stack([c, lax.axis_index("dp")]).astype(jnp.int32)
    seg_blocks = seg_row.reshape(ctx, rows)
    seg = jnp.concatenate([pick(seg_blocks, c ^ r) for r in order]).astype(F32)
    pos = jnp.concatenate([(c ^ r) * rows + jnp.arange(rows, dtype=jnp.int32) for r in order])
    tokens_row = jnp.stack([pos.astype(F32), seg])
    tokens_col = tokens_row.T
    slopes = jnp.exp2(-8.0 * (c * heads + 1 + jnp.arange(heads)).astype(F32) / HEADS)

    ln1_all, qkv_heads, attn_heads, lse, attn_near, attn_far = attention_forward(
        ids, slopes, ln1_parts, full_qkv, qv_bias.reshape(2 * ctx, unit), tokens_col, tokens_row, unit
    )

    def heads_joined(got):
        return jnp.concatenate([got[r] for r in order], axis=0)

    second_full = assemble(None, second, places[:y_count], second_cuts)
    attn_near, attn_far, travel, second_row, out_sends, second_full = lax.optimization_barrier(
        (attn_near, attn_far, travel, second_row, out_sends, second_full)
    )
    pieces = trade(attn_near, attn_far)
    second_full = assemble(second_full, second_row, places[y_count : 2 * y_count], second_cuts)
    second_row = along_y(travel)
    travel = ring_z(travel)
    (out_got,) = assemble(
        None, [g[t] for g in out_sends for t in range(y_count)], places, [lambda b: b[...]]
    )
    out_parts = [col_out, out_got]
    for bit in lower:
        out_parts = gather_step(out_parts, bit)
        cot_parts = gather_step(cot_parts, bit)
    out_parts = [out_parts[slots[r]] for r in range(ctx)]
    attn, middle, normed2, inv_std2, ln2_act = project_out(
        ids, pieces, out_parts, stream, out_bias, ln2_gain, ln2_bias
    )
    ln2_parts = gather_step([ln2_act], top)
    ln2_parts, cot_parts, travel, second_row, second_full = lax.optimization_barrier(
        (ln2_parts, cot_parts, travel, second_row, second_full)
    )
    second_full = assemble(second_full, second_row, places[2 * y_count : 3 * y_count], second_cuts)
    if (z_count, y_count) == (4, 2):
        got = [travel, jnp.stack([ring_y(travel[0]), ring_z(second_row[1][1])])]
    else:
        got = along_y(travel)
    for bit in lower:
        ln2_parts = gather_step(ln2_parts, bit)
    full_up, full_down = assemble(second_full, got, places[3 * y_count :], second_cuts)
    full_up = full_up.reshape(width, dps * sub)
    unit_bias = pick(jnp.moveaxis(up_bias.reshape(dps, ctx, sub), 1, 0), c).reshape(1, dps * sub)
    ln2_all, cot_all, hidden, slope, *grad_down = feed_forward_hidden(
        ids, ln2_parts, full_up, unit_bias, cot_parts, dps
    )
    pre_bf, up_bias_part, ln2_keep, ln2_send = feed_forward_grad(
        ids, slope, full_up, cot_all, full_down
    )
    ln2_keep, ln2_send = scatter_first(ln2_keep, ln2_send)
    ln2_keep, ln2_got = scatter_rest(ln2_keep, ln2_send)
    grad_up = weight_blocks(ids, ln2_all, pre_bf, dps, 2, earlier=[ln2_send])

    down, up = Reduction(grad_down), Reduction(grad_up)
    down_sent = down.step()
    middle_grad, sums2, grad_near, grad_far, col_near, col_far = middle_backward(
        ids,
        ln2_keep,
        ln2_got,
        normed2,
        inv_std2,
        ln2_gain,
        upstream,
        out_parts,
        earlier=[grad_up[0]],
    )
    grad_pieces = trade(grad_near, grad_far)
    cols = trade(*lax.optimization_barrier((col_near, col_far, grad_pieces[2][0]))[:2])
    qkv_bf, qkv_sums, *kinds = attention_backward(
        ids,
        slopes,
        qkv_heads,
        attn_heads,
        grad_pieces,
        lse,
        tokens_col,
        tokens_row,
        unit,
        earlier=[down_sent, down.terms[1][0]],
    )
    cols_got, qkv_bf, *kinds = lax.optimization_barrier(
        ([a for a, _ in cols], qkv_bf, *kinds)
    )
    cols = [(a, i) for a, (_, i) in zip(cols_got, cols)]
    kinds = unit_columns_home(kinds, c)
    ln1_keep, ln1_send, small = input_terms(
        ids, qkv_bf, full_qkv, normed_parts, qkv_sums, sums2, up_bias_part, sub
    )
    while down.bits:
        down.step(ln1_send)
    up.step(ln1_send)
    for bit in reversed(lower):
        small = small + ctx_swap(small, bit)
    ln1_keep, ln1_send = scatter_first(ln1_keep, ln1_send)

    ln1_keep, ln1_send, small, kinds = sync([], ln1_keep, ln1_send, small, kinds)
    qkv = Reduction(unit_blocks(ids, ln1_all, kinds, dps))
    ln1_keep, ln1_got = scatter_rest(ln1_keep, ln1_send)
    small_got = ctx_swap(small, top)

    ln1_got, small_got = sync([down, up], ln1_got, small_got)
    small = small + small_got
    bits = dp_bits()
    small_got = dp_swap(small, bits[0])
    attn_parts = gather_step([attn], top)
    while up.bits:
        up.step()
    input_grad = input_backward(ln1_keep, ln1_got, normed1, inv_std1, ln1_gain, middle_grad)
    result_keep, result_send = scatter_first(*times_weight(hidden, full_down, earlier=[ln1_got]))
    down_home = trade(*down.result(piece_shapes(ctx, sub, unit), column_pieces(ctx)))

    attn_parts, small_got, result_keep, result_send, down_got = sync(
        [up, qkv], attn_parts, small_got, result_keep, result_send, [a for a, _ in down_home]
    )
    down_home = [(a, i) for a, (_, i) in zip(down_got, down_home)]
    qkv.step()
    small = small + small_got
    small_got = dp_swap(small, bits[1])
    for bit in lower:
        attn_parts = gather_step(attn_parts, bit)
    grad_out = out_blocks(ids, attn_parts, cols, dps)
    out = Reduction(grad_out)
    result_keep, result_got = scatter_rest(result_keep, result_send)
    up_rows = w_up.shape[0]
    up_out = up.result(piece_shapes(ctx, up_rows, dps * sub // ctx), column_pieces(ctx))
    up_home = trade(*up_out, grad_out[0])

    up_got, result_got = sync([qkv], [a for a, _ in up_home], result_got)
    up_home = [(a, i) for a, (_, i) in zip(up_got, up_home)]
    while qkv.bits:
        qkv.step()
    out.step()
    shard_up, shard_down = units_home(
        ids, up_home, down_home, w_up.shape, w_down.shape, sub
    )
    result = add_result(middle, result_keep, result_got, down_bias)

    small_got, shard_up, shard_down, result = sync([qkv, out], small_got, shard_up, shard_down, result)
    shard_qkv = qkv.result([(w_qkv.shape, F32)], store_block)[0]
    while out.bits:
        out.step()
    small = small + small_got
    for bit in bits[2:]:
        small = small + dp_swap(small, bit)
    sum_out = out.result([((up_rows, unit), F32)], store_block)[0]

    return (
        result[None],
        input_grad[None],
        small[0],
        small[1],
        shard_qkv,
        small[2:4].reshape(2 * width),
        sum_out,
        small[4],
        small[5],
        small[6],
        shard_up,
        small[8:].reshape(ff),
        shard_down,
        small[7],
    )


def solution(mesh):
    tokens = P("dp", "ctx", None)
    weight = P("dp", "ctx")
    placed = (
        tokens,
        P("dp", None),
        P(),
        P(),
        weight,
        P(),
        weight,
        P(),
        P(),
        P(),
        weight,
        P(),
        weight,
        P(),
        tokens,
    )
    return jax.shard_map(
        per_device,
        mesh=mesh,
        in_specs=placed,
        out_specs=(
            tokens,
            tokens,
            P(),
            P(),
            weight,
            P(),
            weight,
            P(),
            P(),
            P(),
            weight,
            P(),
            weight,
            P(),
        ),
        check_vma=False,
    )
```
